32 devices in a mesh: cast: 4 (over x, core), span: 8 (over z, y).
Axes of the slice: x: 2, y: 2, z: 4, core: 2. Of those that a mesh axis runs over, the one named last changes fastest.
Arguments:
- phase: int32 [16, 64, 1024], P(None, 'cast', 'span'), may hold values from 0 to 2
- viscosity_table: float32 [3], replicated, may hold values from 0.25 to 4
- pressure_source: float32 [16, 64, 1024], P(None, 'cast', 'span'), may hold values from -6 to 6
Outputs:
- solution_field: float32 [16, 64, 1024], P(None, 'cast', 'span')
- residual: float32 [16, 64, 1024], P(None, 'cast', 'span')
The draws below stay inside these ranges and needn't reach their ends.
All inputs are finite; a program needn't handle non-finite values.
Results may differ from the reference program's by a relative error of at most 0.0003.
Values sent between devices are 32-bit elements; how exact they have to be, the bound alone decides.
A program may use at most 64 MiB of HBM per device.

```python
import math
import jax
import jax.numpy as jnp

HZ = 16
LEVELS = 3
PRE = 2
POST = 2
COARSE = 8
NC = 64
NS = 1024


def draw_pressure_source(key, part):
    return jnp.clip(jax.random.normal(key, (HZ, NC, NS), jnp.float32), -6.0, 6.0)


def with_ends(entries, own_key, least, high):
    place = [jax.random.randint(jax.random.fold_in(own_key, axis), (), 0, length) for axis, length in enumerate(entries.shape)]
    longest = entries.shape.index(max(entries.shape))
    beside = place[:longest] + [(place[longest] + 1) % entries.shape[longest]] + place[longest + 1:]
    return entries.at[tuple(place)].set(least).at[tuple(beside)].set(high)


def setup_inputs(seed: int = 0) -> dict:
    arg_keys = jax.random.split(jax.random.key(seed), 4)
    phase = with_ends(jax.random.randint(arg_keys[0], (HZ, NC, NS), 0, 3), jax.random.fold_in(arg_keys[0], 1), 0, 2).astype(jnp.int32)
    viscosity_table = jnp.clip(jnp.exp(jax.random.uniform(arg_keys[1], (3,), jnp.float32, math.log(0.25), math.log(4.0))), 0.25, 4.0)
    pressure_source = draw_pressure_source(jax.random.fold_in(arg_keys[3], 71), 0)
    return dict(phase=phase, viscosity_table=viscosity_table, pressure_source=pressure_source)


relax_weight = 0.8


def harmonic(lower, upper):
    return 2.0 * lower * upper / (lower + upper)


def coarsen(values):
    height, length, width = values.shape
    return jnp.mean(values.reshape(height // 2, 2, length // 2, 2, width // 2, 2), axis=(1, 3, 5))


def refine(values):
    return jnp.repeat(jnp.repeat(jnp.repeat(values, 2, axis=0), 2, axis=1), 2, axis=2)


def face_table(coeff):
    padded = jnp.concatenate([coeff[:, :1], coeff, coeff[:, -1:]], axis=1)
    cast_faces = harmonic(padded[:, :-1], padded[:, 1:])
    span_faces = harmonic(jnp.roll(coeff, 1, axis=2), coeff)
    span_upper = jnp.roll(span_faces, -1, axis=2)
    flat = jnp.zeros_like(coeff[:1])
    height_faces = jnp.concatenate([flat, harmonic(coeff[:-1], coeff[1:]), flat], axis=0)
    diagonal = cast_faces[:, :-1] + cast_faces[:, 1:] + span_faces + span_upper + height_faces[:-1] + height_faces[1:]
    return cast_faces, span_faces, span_upper, height_faces, diagonal


def operate(values, table, scale):
    cast_faces, span_faces, span_upper, height_faces, diagonal = table
    zero_cast = jnp.zeros_like(values[:, :1])
    zero_height = jnp.zeros_like(values[:1])
    cast_below = jnp.concatenate([zero_cast, values[:, :-1]], axis=1)
    cast_above = jnp.concatenate([values[:, 1:], zero_cast], axis=1)
    below = jnp.concatenate([zero_height, values[:-1]], axis=0)
    above = jnp.concatenate([values[1:], zero_height], axis=0)
    near = (cast_faces[:, :-1] * cast_below + cast_faces[:, 1:] * cast_above
            + span_faces * jnp.roll(values, 1, axis=2) + span_upper * jnp.roll(values, -1, axis=2)
            + height_faces[:-1] * below + height_faces[1:] * above)
    return scale * (diagonal * values - near)


def relax(values, source, table, scale):
    return values + relax_weight * (source - operate(values, table, scale)) / (scale * table[4])


def reference(phase, viscosity_table, pressure_source):
    viscosity = jnp.where(phase == 0, viscosity_table[0], jnp.where(phase == 1, viscosity_table[1], viscosity_table[2]))
    coeff = 1.0 / viscosity
    tables = []
    for level in range(LEVELS + 1):
        tables.append(face_table(coeff))
        if level < LEVELS:
            coeff = coarsen(coeff)
    sources = [pressure_source]
    kept = []
    for level in range(LEVELS):
        scale = 0.25 ** level
        values = jnp.zeros_like(sources[level])
        for sweep in range(PRE):
            values = relax(values, sources[level], tables[level], scale)
        remainder = sources[level] - operate(values, tables[level], scale)
        kept.append(values)
        sources.append(coarsen(remainder))
    scale = 0.25 ** LEVELS
    values = jnp.zeros_like(sources[LEVELS])
    for sweep in range(COARSE):
        values = relax(values, sources[LEVELS], tables[LEVELS], scale)
    for level in reversed(range(LEVELS)):
        scale = 0.25 ** level
        values = kept[level] + refine(values)
        for sweep in range(POST):
            values = relax(values, sources[level], tables[level], scale)
    residual = pressure_source - operate(values, tables[0], 1.0)
    return values, residual
```

```python
import functools
import jax
import jax.numpy as jnp
from jax import lax
from jax.experimental import pallas as pl
from jax.experimental.pallas import tpu as pltpu
from jax.sharding import PartitionSpec as P

LEVELS = 3
PRE = 2
POST = 2
COARSE = 8
PAD = 8
LANES = 128

relax_weight = 0.8
MESH = pl.DeviceIdType.MESH


def harmonic(a, b):
    return 2.0 * a * b / (a + b)


def lane_iota(rows):
    return lax.broadcasted_iota(jnp.int32, (rows, LANES), 1)


def from_lower(tiles):
    rolled = [pltpu.roll(v, 1, 1) for v in tiles]
    if len(tiles) == 1:
        return rolled
    edge = lane_iota(tiles[0].shape[0]) == 0
    return [jnp.where(edge, rolled[t - 1], rolled[t]) for t in range(len(tiles))]


def from_upper(tiles):
    rolled = [pltpu.roll(v, LANES - 1, 1) for v in tiles]
    if len(tiles) == 1:
        return rolled
    edge = lane_iota(tiles[0].shape[0]) == LANES - 1
    n = len(tiles)
    return [jnp.where(edge, rolled[(t + 1) % n], rolled[t]) for t in range(n)]


def select_mm(values, matrix):
    high = values.astype(jnp.bfloat16)
    low = (values - high.astype(jnp.float32)).astype(jnp.bfloat16)
    return jnp.dot(high, matrix, preferred_element_type=jnp.float32) + jnp.dot(
        low, matrix, preferred_element_type=jnp.float32
    )


def as_matrix(mask):
    return jnp.where(mask, 1.0, 0.0).astype(jnp.bfloat16)


class Level:
    def __init__(self, tiles, height, rows, unroll):
        self.tiles, self.height, self.rows, self.unroll = tiles, height, rows, unroll

    def scratch(self):
        t, h, r = self.tiles, self.height, self.rows
        grown = r + 2 * PAD
        field = pltpu.VMEM((t, h, r, LANES), jnp.float32)
        return [
            pltpu.VMEM((2, t, h, grown, LANES), jnp.float32),
            pltpu.VMEM((t, h + 2, grown, LANES), jnp.float32),
            pltpu.VMEM((t, h + 2, grown, LANES), jnp.float32),
            field, field, field, field,
            pltpu.VMEM((t, h + 1, r, LANES), jnp.float32),
            field, field,
            field,
        ]

    def bind(self, refs):
        (self.cb, self.xa, self.xb, self.cl, self.cu, self.sl, self.su, self.fh,
         self.diag, self.weight, self.rem) = refs

    def loop(self, body):
        if self.unroll:
            for h in range(self.height):
                body(h)
        else:
            def step(h, carry):
                body(h)
                return carry
            lax.fori_loop(0, self.height, step, 0)

    def clear_pads(self):
        t, h, r = self.tiles, self.height, self.rows
        for x in (self.xa, self.xb):
            x[:, :, 0:PAD, :] = jnp.zeros((t, h + 2, PAD, LANES), jnp.float32)
            x[:, :, PAD + r:, :] = jnp.zeros((t, h + 2, PAD, LANES), jnp.float32)
            x[:, 0:1, PAD:PAD + r, :] = jnp.zeros((t, 1, r, LANES), jnp.float32)
            x[:, h + 1:h + 2, PAD:PAD + r, :] = jnp.zeros((t, 1, r, LANES), jnp.float32)
        self.fh[:, 0:1] = jnp.zeros((t, 1, r, LANES), jnp.float32)

    def clear_coeff_pads(self):
        t, h, r = self.tiles, self.height, self.rows
        self.cb[0, :, :, 0:PAD, :] = jnp.ones((t, h, PAD, LANES), jnp.float32)
        self.cb[0, :, :, PAD + r:, :] = jnp.ones((t, h, PAD, LANES), jnp.float32)

    def prepare(self, first_row, total_rows):
        t_n, h_n, r = self.tiles, self.height, self.rows
        place = lax.broadcasted_iota(jnp.int32, (r, LANES), 0) + first_row
        at_start = place == 0
        at_stop = place == total_rows - 1
        outside = place == total_rows
        below = place == -1

        def body(h):
            coeff = [self.cb[0, t, h, PAD:PAD + r, :] for t in range(t_n)]
            span_lower = [harmonic(a, b) for a, b in zip(from_lower(coeff), coeff)]
            span_upper = from_upper(span_lower)
            top = min(h + 1, h_n - 1) if self.unroll else jnp.minimum(h + 1, h_n - 1)
            for t in range(t_n):
                c = coeff[t]
                lower = harmonic(self.cb[0, t, h, PAD - 1:PAD - 1 + r, :], c)
                upper = harmonic(c, self.cb[0, t, h, PAD + 1:PAD + 1 + r, :])
                self.cl[t, h] = jnp.where(at_start | outside, 0.0, lower)
                self.cu[t, h] = jnp.where(at_stop | below, 0.0, upper)
                lower = jnp.where(at_start, c, lower)
                upper = jnp.where(at_stop, c, upper)
                self.sl[t, h] = span_lower[t]
                self.su[t, h] = span_upper[t]
                height_upper = harmonic(c, self.cb[0, t, top, PAD:PAD + r, :])
                height_upper = jnp.where(h < h_n - 1, height_upper, 0.0)
                self.fh[t, h + 1] = height_upper
                diagonal = (lower + upper + span_lower[t] + span_upper[t]
                            + self.fh[t, h] + height_upper)
                weight = relax_weight / diagonal
                self.diag[t, h] = diagonal
                self.weight[t, h] = weight
                self.xa[t, h + 1, PAD:PAD + r, :] = weight * self.cb[1, t, h, PAD:PAD + r, :]
        self.loop(body)

    def near(self, x, h, start, n, tiles):
        centre = [x[t, h + 1, pl.ds(PAD + start, n), :] for t in range(self.tiles)]
        lower, upper = from_lower(centre), from_upper(centre)
        rows = pl.ds(start, n)
        out = []
        for t in range(tiles):
            out.append(
                self.cl[t, h, rows, :] * x[t, h + 1, pl.ds(PAD - 1 + start, n), :]
                + self.cu[t, h, rows, :] * x[t, h + 1, pl.ds(PAD + 1 + start, n), :]
                + self.sl[t, h, rows, :] * lower[t]
                + self.su[t, h, rows, :] * upper[t]
                + self.fh[t, h, rows, :] * x[t, h, pl.ds(PAD + start, n), :]
                + self.fh[t, h + 1, rows, :] * x[t, h + 2, pl.ds(PAD + start, n), :]
                + self.cb[1, t, h, pl.ds(PAD + start, n), :]
            )
        return centre, out

    def relax(self, x, y, start, n):
        def body(h):
            centre, near = self.near(x, h, start, n, self.tiles)
            for t in range(self.tiles):
                y[t, h + 1, pl.ds(PAD + start, n), :] = (
                    (1.0 - relax_weight) * centre[t] + self.weight[t, h, pl.ds(start, n), :] * near[t]
                )
        self.loop(body)

    def remainder(self, x, start, n, tiles, store):
        def body(h):
            centre, near = self.near(x, h, start, n, tiles)
            for t in range(tiles):
                store(t, h, near[t] - self.diag[t, h, pl.ds(start, n), :] * centre[t], centre[t])
        self.loop(body)

    def keep_remainder(self, x, start, n):
        def store(t, h, value, centre):
            self.rem[t, h, pl.ds(start, n), :] = value
        self.remainder(x, start, n, self.tiles, store)


def coarsen(fine, coarse):
    half = fine.rows // 2
    key, lane = (lax.broadcasted_iota(jnp.int32, (LANES, LANES), d) for d in (0, 1))
    into = [as_matrix(lane == (key >> 1)), as_matrix(lane == 64 + (key >> 1))]
    for t in range(coarse.tiles):
        total = None
        for side in range(2):
            f = 2 * t + side
            parts = []
            for h in range(coarse.height):
                part = None
                for plane in (2 * h, 2 * h + 1):
                    for odd in range(2):
                        piece = fine.cb[0, f, plane, pl.ds(PAD + odd, half, stride=2), :]
                        part = piece if part is None else part + piece
                parts.append(part * (0.125 * 0.25))
            for h in range(coarse.height):
                part = None
                for plane in (2 * h, 2 * h + 1):
                    for odd in range(2):
                        piece = fine.rem[f, plane, pl.ds(odd, half, stride=2), :]
                        part = piece if part is None else part + piece
                parts.append(part * 0.125)
            product = select_mm(jnp.concatenate(parts, axis=0), into[side])
            total = product if total is None else total + product
        coarse.cb[:, t, :, PAD:PAD + half, :] = total.reshape(2, coarse.height, half, LANES)


def refine_add(coarse, x, fine, y, z, wide):
    half = fine.rows // 2
    key, lane = (lax.broadcasted_iota(jnp.int32, (LANES, LANES), d) for d in (0, 1))
    out_of = [as_matrix(key == (lane >> 1)), as_matrix(key == 64 + (lane >> 1))]
    for t in range(coarse.tiles):
        stacked = x[t, 1:1 + coarse.height, PAD:PAD + half, :].reshape(coarse.height * half, LANES)
        for side in range(2):
            f = 2 * t + side
            product = select_mm(stacked, out_of[side]).reshape(coarse.height, half, LANES)
            for h in range(coarse.height):
                for odd in range(2):
                    wide[h, pl.ds(odd, half, stride=2), :] = product[h]
            for h in range(coarse.height):
                rows = wide[h, 0:fine.rows, :]
                for plane in (2 * h, 2 * h + 1):
                    z[f, plane + 1, PAD:PAD + fine.rows, :] = y[f, plane + 1, PAD:PAD + fine.rows, :] + rows


def kernel(n_cast, n_span, levels, table_ref, phase_ref, source_ref, field_ref, residual_ref, *scratch):
    for i, level in enumerate(levels):
        level.bind(scratch[11 * i:11 * i + 11])
    l0, l1, l2, l3 = levels
    (edges, halos, small, packed, gathered, tall, wide0, wide2,
     send_sem, recv_sem, send_c, recv_c, send_s, recv_s) = scratch[44:]
    c, s = lax.axis_index("cast"), lax.axis_index("span")
    height, rows, _ = phase_ref.shape
    own = slice(PAD + rows, PAD + 2 * rows)

    def span_at(offset):
        return lax.rem(s + offset + n_span, n_span)

    def cast_at(offset):
        return lax.rem(c + offset + n_cast, n_cast)

    l0.clear_coeff_pads()

    def blank(block):
        at = slice(PAD + block * rows, PAD + (block + 1) * rows)
        l0.cb[0, 0, :, at, :] = jnp.ones((height, rows, LANES), jnp.float32)
        l0.cb[1, 0, :, at, :] = jnp.zeros((height, rows, LANES), jnp.float32)
        within = slice(block * rows, (block + 1) * rows)
        for side in range(2):
            halos[side, 0, :, within, :] = jnp.ones((2, rows, LANES), jnp.float32)
            halos[side, 1, :, within, :] = jnp.zeros((2, rows, LANES), jnp.float32)

    @pl.when(c == 0)
    def _():
        blank(0)

    @pl.when(c == n_cast - 1)
    def _():
        blank(2)

    barrier = pltpu.get_barrier_semaphore()

    def greet(cast, span):
        pl.semaphore_signal(barrier, inc=1, device_id=(cast, span), device_id_type=MESH)

    for d in range(1, n_cast):
        greet(cast_at(d), s)
    for d in range(1, n_span):
        greet(c, span_at(d))

    @pl.when(c > 0)
    def _():
        greet(c - 1, span_at(1))
        greet(c - 1, span_at(-1))

    @pl.when(c < n_cast - 1)
    def _():
        greet(c + 1, span_at(1))
        greet(c + 1, span_at(-1))

    phase = phase_ref[...]
    v0, v1, v2 = table_ref[0], table_ref[1], table_ref[2]
    l0.cb[0, 0, :, own, :] = 1.0 / jnp.where(phase == 0, v0, jnp.where(phase == 1, v1, v2))
    l0.cb[1, 0, :, own, :] = source_ref[...]
    group = lane_iota(rows) >> 4
    for kind in range(2):
        for part in range(2):
            planes = [l0.cb[kind, 0, 8 * part + j, own, :] for j in range(8)]
            for side in range(2):
                merged = planes[0] if side == 0 else pltpu.roll(planes[0], 16, 1)
                for j in range(1, 8):
                    shift = (16 * j + 16 * side) % LANES
                    moved = pltpu.roll(planes[j], shift, 1) if shift else planes[j]
                    merged = jnp.where(group == j, moved, merged)
                edges[side, kind, part] = merged

    has_lower = lax.div(c + n_cast - 1, n_cast)
    has_upper = lax.div(2 * n_cast - 2 - c, n_cast)
    pl.semaphore_wait(barrier, n_cast + n_span - 2 + 2 * has_lower + 2 * has_upper)

    def block_copy(dc):
        block = 1 - dc
        return pltpu.make_async_remote_copy(
            src_ref=l0.cb.at[:, 0, :, pl.ds(PAD + rows, rows), :],
            dst_ref=l0.cb.at[:, 0, :, pl.ds(PAD + block * rows, rows), :],
            send_sem=send_sem.at[6 + (dc + 1) // 2],
            recv_sem=recv_sem.at[6 + (dc + 1) // 2],
            device_id=(c + dc, s),
            device_id_type=MESH,
        )

    def edge_copy(dc, side):
        return pltpu.make_async_remote_copy(
            src_ref=edges.at[side],
            dst_ref=halos.at[side, :, :, pl.ds((1 - dc) * rows, rows), :],
            send_sem=send_sem.at[3 * side + dc + 1],
            recv_sem=recv_sem.at[3 * side + dc + 1],
            device_id=(c + dc, span_at(2 * side - 1)),
            device_id_type=MESH,
        )

    @pl.when(c < n_cast - 1)
    def _():
        block_copy(1).start()
        edge_copy(1, 0).start()
        edge_copy(1, 1).start()

    @pl.when(c > 0)
    def _():
        block_copy(-1).start()
        edge_copy(-1, 0).start()
        edge_copy(-1, 1).start()

    edge_copy(0, 0).start()
    edge_copy(0, 1).start()

    for level in levels:
        level.clear_pads()
    for level in levels[1:]:
        level.clear_coeff_pads()
    tall[...] = jnp.zeros(tall.shape, jnp.float32)

    edge_copy(0, 0).wait()
    edge_copy(0, 1).wait()

    @pl.when(c > 0)
    def _():
        block_copy(1).wait_recv()
        edge_copy(1, 0).wait_recv()
        edge_copy(1, 1).wait_recv()
        block_copy(-1).wait_send()
        edge_copy(-1, 0).wait_send()
        edge_copy(-1, 1).wait_send()

    @pl.when(c < n_cast - 1)
    def _():
        block_copy(-1).wait_recv()
        edge_copy(-1, 0).wait_recv()
        edge_copy(-1, 1).wait_recv()
        block_copy(1).wait_send()
        edge_copy(1, 0).wait_send()
        edge_copy(1, 1).wait_send()

    first_half = lane_iota(3 * rows) < 64
    for kind in range(2):
        for part in range(2):
            above, beneath = halos[0, kind, part], halos[1, kind, part]
            for j in range(8):
                a = pltpu.roll(above, (LANES - 16 * j) % LANES, 1) if j else above
                b = pltpu.roll(beneath, 112 - 16 * j, 1) if j < 7 else beneath
                l0.cb[kind, 1, 8 * part + j, PAD:PAD + 3 * rows, :] = jnp.where(first_half, a, b)

    l0.prepare(rows * c - rows, rows * n_cast)
    l0.relax(l0.xa, l0.xb, 0, 3 * rows)
    l0.keep_remainder(l0.xb, 0, 3 * rows)
    coarsen(l0, l1)
    rows1 = rows // 2
    l1.prepare(rows1 * c - rows1, rows1 * n_cast)
    l1.relax(l1.xa, l1.xb, 0, 3 * rows1)
    l1.keep_remainder(l1.xb, rows1, rows1)

    rows2 = rows1 // 2
    for h in range(l2.height):
        for k in range(2):
            part = None
            for plane in (2 * h, 2 * h + 1):
                for odd in range(2):
                    if k == 0:
                        piece = l1.rem[0, plane, pl.ds(rows1 + odd, rows2, stride=2), :]
                    else:
                        piece = l1.cb[0, 0, plane, pl.ds(PAD + rows1 + odd, rows2, stride=2), :]
                    part = piece if part is None else part + piece
            small[h, rows2 * k:rows2 * (k + 1), :] = part * (0.125 if k == 0 else 0.125 * 0.25)
    key, lane = (lax.broadcasted_iota(jnp.int32, (LANES, LANES), d) for d in (0, 1))
    product = select_mm(small[...].reshape(8 * l2.height, LANES), as_matrix((lane == (key >> 1)) & (key < 64)))
    product = product.reshape(l2.height, 8, LANES)
    merged = product[0]
    for h in range(1, l2.height):
        merged = merged + pltpu.roll(product[h], 32 * h, 1)
    packed[...] = merged
    gathered[s, c] = merged

    copies = []
    for d in range(1, n_cast):
        copies.append(pltpu.make_async_remote_copy(
            src_ref=packed, dst_ref=gathered.at[s, c], send_sem=send_c.at[d - 1], recv_sem=recv_c.at[d - 1],
            device_id=(cast_at(d), s), device_id_type=MESH))
        copies[-1].start()
    for copy in copies:
        copy.wait()
    copies = []
    for d in range(1, n_span):
        copies.append(pltpu.make_async_remote_copy(
            src_ref=gathered.at[s], dst_ref=gathered.at[s], send_sem=send_s.at[d - 1], recv_sem=recv_s.at[d - 1],
            device_id=(c, span_at(d)), device_id_type=MESH))
        copies[-1].start()
    for copy in copies:
        copy.wait()

    quarter = lane_iota(8) >> 5
    for t in range(l2.tiles):
        for cc in range(n_cast):
            blocks = [gathered[4 * t + j, cc] for j in range(4)]
            for h in range(l2.height):
                joined = None
                for j in range(4):
                    shift = (32 * (j - h)) % LANES
                    moved = pltpu.roll(blocks[j], shift, 1) if shift else blocks[j]
                    joined = moved if joined is None else jnp.where(quarter == j, moved, joined)
                at = PAD + rows2 * cc
                l2.cb[1, t, h, at:at + rows2, :] = joined[:rows2]
                l2.cb[0, t, h, at:at + rows2, :] = joined[rows2:]

    l2.prepare(0, l2.rows)
    l2.relax(l2.xa, l2.xb, 0, l2.rows)
    l2.keep_remainder(l2.xb, 0, l2.rows)
    coarsen(l2, l3)
    l3.prepare(0, l3.rows)
    x, y = l3.xa, l3.xb
    for _ in range(COARSE - 1):
        l3.relax(x, y, 0, l3.rows)
        x, y = y, x
    refine_add(l3, x, l2, l2.xb, l2.xa, wide2)
    l2.relax(l2.xa, l2.xb, 0, l2.rows)
    l2.relax(l2.xb, l2.xa, 0, l2.rows)

    period = 64 * n_span
    place = jnp.where(lane < 96, lane, lane - LANES) + 64 * s
    place = jnp.where(place < 0, place + period, jnp.where(place >= period, place - period, place)) >> 1
    product = None
    for t in range(l2.tiles):
        stacked = l2.xa[t, 1:1 + l2.height, PAD:PAD + l2.rows, :].reshape(l2.height * l2.rows, LANES)
        term = select_mm(stacked, as_matrix(key + LANES * t == place))
        product = term if product is None else product + term
    product = product.reshape(l2.height, l2.rows, LANES)
    for h in range(l2.height):
        for odd in range(2):
            tall[h, pl.ds(PAD + odd, l2.rows, stride=2), :] = product[h]
    for h in range(l2.height):
        window = tall[h, pl.ds(pl.multiple_of(8 * c, 8), 3 * rows1), :]
        for plane in (2 * h, 2 * h + 1):
            l1.xa[0, plane + 1, PAD:PAD + 3 * rows1, :] = l1.xb[0, plane + 1, PAD:PAD + 3 * rows1, :] + window
    l1.relax(l1.xa, l1.xb, 0, 3 * rows1)
    l1.relax(l1.xb, l1.xa, 0, 3 * rows1)
    refine_add(l1, l1.xa, l0, l0.xb, l0.xa, wide0)
    l0.relax(l0.xa, l0.xb, rows - 8, rows + 16)
    l0.relax(l0.xb, l0.xa, rows - 8, rows + 16)

    def finish(t, h, value, centre):
        field_ref[h] = centre
        residual_ref[h] = value

    l0.remainder(l0.xa, rows, rows, 1, finish)


def solution(mesh):
    n_cast, n_span = mesh.shape["cast"], mesh.shape["span"]

    def shards(phase, viscosity_table, pressure_source):
        height, rows, width = phase.shape
        assert (height, rows, width) == (16, 16, LANES)
        levels = [
            Level(2, 16, 3 * rows, False),
            Level(1, 8, 3 * rows // 2, False),
            Level(n_span // 4, 4, 4 * n_cast, True),
            Level(n_span // 8, 2, 2 * n_cast, True),
        ]
        scratch = []
        for level in levels:
            scratch += level.scratch()
        dma = pltpu.SemaphoreType.DMA
        scratch += [
            pltpu.VMEM((2, 2, 2, rows, LANES), jnp.float32),
            pltpu.VMEM((2, 2, 2, 3 * rows, LANES), jnp.float32),
            pltpu.VMEM((4, 8, LANES), jnp.float32),
            pltpu.VMEM((8, LANES), jnp.float32),
            pltpu.VMEM((n_span, n_cast, 8, LANES), jnp.float32),
            pltpu.VMEM((4, 8 * n_cast + 2 * PAD, LANES), jnp.float32),
            pltpu.VMEM((8, 3 * rows, LANES), jnp.float32),
            pltpu.VMEM((2, 4 * n_cast, LANES), jnp.float32),
            dma((8,)), dma((8,)),
            dma((n_cast - 1,)), dma((n_cast - 1,)),
            dma((n_span - 1,)), dma((n_span - 1,)),
        ]
        block = jax.ShapeDtypeStruct(phase.shape, jnp.float32)
        vmem = pl.BlockSpec(memory_space=pltpu.VMEM)
        return pl.pallas_call(
            functools.partial(kernel, n_cast, n_span, levels),
            out_shape=(block, block),
            in_specs=[pl.BlockSpec(memory_space=pltpu.SMEM), vmem, vmem],
            out_specs=(vmem, vmem),
            scratch_shapes=scratch,
            compiler_params=pltpu.CompilerParams(
                collective_id=0, has_side_effects=True, vmem_limit_bytes=48 * 2**20
            ),
        )(viscosity_table, phase, pressure_source)

    placed = P(None, "cast", "span")
    return jax.shard_map(
        shards, mesh=mesh, in_specs=(placed, P(), placed), out_specs=(placed, placed), check_vma=False
    )
```

```python
import functools
import jax
import jax.numpy as jnp
from jax import lax
from jax.experimental import pallas as pl
from jax.experimental.pallas import tpu as pltpu
from jax.sharding import PartitionSpec as P

LEVELS = 3
PRE = 2
POST = 2
COARSE = 8
PAD = 8
LANES = 128

relax_weight = 0.8
MESH = pl.DeviceIdType.MESH


def harmonic(a, b):
    return 2.0 * a * b / (a + b)


def lane_iota(rows):
    return lax.broadcasted_iota(jnp.int32, (rows, LANES), 1)


def from_lower(tiles):
    rolled = [pltpu.roll(v, 1, 1) for v in tiles]
    if len(tiles) == 1:
        return rolled
    edge = lane_iota(tiles[0].shape[0]) == 0
    return [jnp.where(edge, rolled[t - 1], rolled[t]) for t in range(len(tiles))]


def from_upper(tiles):
    rolled = [pltpu.roll(v, LANES - 1, 1) for v in tiles]
    if len(tiles) == 1:
        return rolled
    edge = lane_iota(tiles[0].shape[0]) == LANES - 1
    n = len(tiles)
    return [jnp.where(edge, rolled[(t + 1) % n], rolled[t]) for t in range(n)]


def select_mm(values, matrix):
    high = values.astype(jnp.bfloat16)
    low = (values - high.astype(jnp.float32)).astype(jnp.bfloat16)
    return jnp.dot(high, matrix, preferred_element_type=jnp.float32) + jnp.dot(
        low, matrix, preferred_element_type=jnp.float32
    )


def as_matrix(mask):
    return jnp.where(mask, 1.0, 0.0).astype(jnp.bfloat16)


class Level:
    def __init__(self, tiles, height, rows, unroll):
        self.tiles, self.height, self.rows, self.unroll = tiles, height, rows, unroll

    def scratch(self):
        t, h, r = self.tiles, self.height, self.rows
        grown = r + 2 * PAD
        field = pltpu.VMEM((t, h, r, LANES), jnp.float32)
        return [
            pltpu.VMEM((2, t, h, grown, LANES), jnp.float32),
            pltpu.VMEM((t, h + 2, grown, LANES), jnp.float32),
            pltpu.VMEM((t, h + 2, grown, LANES), jnp.float32),
            pltpu.VMEM((t, h, r + PAD, LANES), jnp.float32),
            field, field,
            pltpu.VMEM((t, h + 1, r, LANES), jnp.float32),
            field, field,
            field,
        ]

    def bind(self, refs):
        (self.cb, self.xa, self.xb, self.cl, self.sl, self.su, self.fh,
         self.diag, self.weight, self.rem) = refs

    def loop(self, body):
        def step(i, carry):
            for k in range(self.unroll):
                body(i * self.unroll + k, k)
            return carry
        if self.unroll == self.height:
            step(0, 0)
        else:
            lax.fori_loop(0, self.height // self.unroll, step, 0)

    def clear_pads(self):
        t, h, r = self.tiles, self.height, self.rows
        for x in (self.xa, self.xb):
            x[:, :, 0:PAD, :] = jnp.zeros((t, h + 2, PAD, LANES), jnp.float32)
            x[:, :, PAD + r:, :] = jnp.zeros((t, h + 2, PAD, LANES), jnp.float32)
            x[:, 0:1, PAD:PAD + r, :] = jnp.zeros((t, 1, r, LANES), jnp.float32)
            x[:, h + 1:h + 2, PAD:PAD + r, :] = jnp.zeros((t, 1, r, LANES), jnp.float32)
        self.cl[:, :, r:, :] = jnp.zeros((t, h, PAD, LANES), jnp.float32)
        self.fh[:, 0:1] = jnp.zeros((t, 1, r, LANES), jnp.float32)

    def clear_coeff_pads(self):
        t, h, r = self.tiles, self.height, self.rows
        self.cb[0, :, :, 0:PAD, :] = jnp.ones((t, h, PAD, LANES), jnp.float32)
        self.cb[0, :, :, PAD + r:, :] = jnp.ones((t, h, PAD, LANES), jnp.float32)

    def prepare(self, first_row, total_rows):
        t_n, h_n, r = self.tiles, self.height, self.rows
        place = lax.broadcasted_iota(jnp.int32, (r, LANES), 0) + first_row
        at_start = place == 0
        at_stop = place == total_rows - 1
        at_wall = at_start | (place == total_rows)
        held = {}

        def body(h, k):
            coeff = [self.cb[0, t, h, PAD:PAD + r, :] for t in range(t_n)]
            span_lower = [harmonic(a, b) for a, b in zip(from_lower(coeff), coeff)]
            span_upper = from_upper(span_lower)
            top = min(h + 1, h_n - 1) if self.unroll == h_n else jnp.minimum(h + 1, h_n - 1)
            for t in range(t_n):
                c = coeff[t]
                lower = harmonic(self.cb[0, t, h, PAD - 1:PAD - 1 + r, :], c)
                lower = jnp.where(at_wall, 0.0, lower)
                self.cl[t, h, 0:r, :] = lower
                upper = self.cl[t, h, 1:1 + r, :]
                lower = jnp.where(at_start, c, lower)
                upper = jnp.where(at_stop, c, upper)
                self.sl[t, h] = span_lower[t]
                self.su[t, h] = span_upper[t]
                height_upper = harmonic(c, self.cb[0, t, top, PAD:PAD + r, :])
                height_upper = jnp.where(h < h_n - 1, height_upper, 0.0)
                height_lower = held[t] if k else self.fh[t, h]
                held[t] = height_upper
                self.fh[t, h + 1] = height_upper
                diagonal = (lower + upper + span_lower[t] + span_upper[t]
                            + height_lower + height_upper)
                self.diag[t, h] = diagonal
                self.weight[t, h] = relax_weight / diagonal
        self.loop(body)

    def begin(self):
        r = self.rows

        def body(h, k):
            for t in range(self.tiles):
                self.xa[t, h + 1, PAD:PAD + r, :] = self.weight[t, h] * self.cb[1, t, h, PAD:PAD + r, :]
        self.loop(body)

    def near(self, x, h, start, n, tiles):
        centre = [x[t, h + 1, pl.ds(PAD + start, n), :] for t in range(self.tiles)]
        lower, upper = from_lower(centre), from_upper(centre)
        rows = pl.ds(start, n)
        out = []
        for t in range(tiles):
            out.append(
                self.cl[t, h, rows, :] * x[t, h + 1, pl.ds(PAD - 1 + start, n), :]
                + self.cl[t, h, pl.ds(start + 1, n), :] * x[t, h + 1, pl.ds(PAD + 1 + start, n), :]
                + self.sl[t, h, rows, :] * lower[t]
                + self.su[t, h, rows, :] * upper[t]
                + self.fh[t, h, rows, :] * x[t, h, pl.ds(PAD + start, n), :]
                + self.fh[t, h + 1, rows, :] * x[t, h + 2, pl.ds(PAD + start, n), :]
                + self.cb[1, t, h, pl.ds(PAD + start, n), :]
            )
        return centre, out

    def relax(self, x, y, start, n):
        def body(h, k):
            centre, near = self.near(x, h, start, n, self.tiles)
            for t in range(self.tiles):
                y[t, h + 1, pl.ds(PAD + start, n), :] = (
                    (1.0 - relax_weight) * centre[t] + self.weight[t, h, pl.ds(start, n), :] * near[t]
                )
        self.loop(body)

    def remainder(self, x, start, n, tiles, store):
        def body(h, k):
            centre, near = self.near(x, h, start, n, tiles)
            for t in range(tiles):
                store(t, h, near[t] - self.diag[t, h, pl.ds(start, n), :] * centre[t], centre[t])
        self.loop(body)

    def keep_remainder(self, x, start, n):
        def store(t, h, value, centre):
            self.rem[t, h, pl.ds(start, n), :] = value
        self.remainder(x, start, n, self.tiles, store)


def children(pieces):
    total = None
    for piece in pieces:
        total = piece if total is None else total + piece
    return total


def coarsen(fine, coarse, kind):
    half = fine.rows // 2
    key, lane = (lax.broadcasted_iota(jnp.int32, (LANES, LANES), d) for d in (0, 1))
    into = [as_matrix(lane == (key >> 1)), as_matrix(lane == 64 + (key >> 1))]
    ref, first = (fine.cb.at[0], PAD) if kind == 0 else (fine.rem, 0)
    scale = 0.125 * 0.25 if kind == 0 else 0.125
    for t in range(coarse.tiles):
        total = None
        for side in range(2):
            parts = [
                children(
                    ref[2 * t + side, plane, pl.ds(first + odd, half, stride=2), :]
                    for plane in (2 * h, 2 * h + 1) for odd in range(2)
                ) * scale
                for h in range(coarse.height)
            ]
            product = select_mm(jnp.concatenate(parts, axis=0), into[side])
            total = product if total is None else total + product
        coarse.cb[kind, t, :, PAD:PAD + half, :] = total.reshape(coarse.height, half, LANES)


def refine_add(coarse, x, fine, y, z, wide):
    half = fine.rows // 2
    key, lane = (lax.broadcasted_iota(jnp.int32, (LANES, LANES), d) for d in (0, 1))
    out_of = [as_matrix(key == (lane >> 1)), as_matrix(key == 64 + (lane >> 1))]
    for t in range(coarse.tiles):
        stacked = x[t, 1:1 + coarse.height, PAD:PAD + half, :].reshape(coarse.height * half, LANES)
        for side in range(2):
            f = 2 * t + side
            product = select_mm(stacked, out_of[side]).reshape(coarse.height, half, LANES)
            for h in range(coarse.height):
                for odd in range(2):
                    wide[h, pl.ds(odd, half, stride=2), :] = product[h]
            for h in range(coarse.height):
                rows = wide[h, 0:fine.rows, :]
                for plane in (2 * h, 2 * h + 1):
                    z[f, plane + 1, PAD:PAD + fine.rows, :] = y[f, plane + 1, PAD:PAD + fine.rows, :] + rows


def kernel(n_cast, n_span, levels, table_ref, phase_hbm, source_hbm, field_ref, residual_ref, *scratch):
    for i, level in enumerate(levels):
        level.bind(scratch[10 * i:10 * i + 10])
    l0, l1, l2, l3 = levels
    (phase_ref, edges, halos, half, small, packed, gathered, tall, wide0, wide2, load_sem,
     send_sem, recv_sem, send_c, recv_c, send_s, recv_s) = scratch[40:]
    c, s = lax.axis_index("cast"), lax.axis_index("span")
    height, rows, _ = phase_ref.shape
    rows1, rows2 = rows // 2, rows // 4
    own = slice(PAD + rows, PAD + 2 * rows)
    load_phase = pltpu.make_async_copy(phase_hbm, phase_ref, load_sem.at[0])
    load_source = pltpu.make_async_copy(source_hbm, l0.cb.at[1, 0, :, own, :], load_sem.at[1])
    load_phase.start()
    load_source.start()

    def span_at(offset):
        return lax.rem(s + offset + n_span, n_span)

    def cast_at(offset):
        return lax.rem(c + offset + n_cast, n_cast)

    def blank(block):
        at = slice(PAD + block * rows, PAD + (block + 1) * rows)
        l0.cb[0, 0, :, at, :] = jnp.ones((height, rows, LANES), jnp.float32)
        l0.cb[1, 0, :, at, :] = jnp.zeros((height, rows, LANES), jnp.float32)
        within = slice(block * rows, (block + 1) * rows)
        for side in range(2):
            halos[0, side, :, within, :] = jnp.ones((2, rows, LANES), jnp.float32)
            halos[1, side, :, within, :] = jnp.zeros((2, rows, LANES), jnp.float32)

    @pl.when(c == 0)
    def _():
        blank(0)

    @pl.when(c == n_cast - 1)
    def _():
        blank(2)

    barrier = pltpu.get_barrier_semaphore()

    def greet(cast, span):
        pl.semaphore_signal(barrier, inc=1, device_id=(cast, span), device_id_type=MESH)

    for d in range(1, n_cast):
        greet(cast_at(d), s)
    for d in range(1, n_span):
        greet(c, span_at(d))

    @pl.when(c > 0)
    def _():
        greet(c - 1, span_at(1))
        greet(c - 1, span_at(-1))

    @pl.when(c < n_cast - 1)
    def _():
        greet(c + 1, span_at(1))
        greet(c + 1, span_at(-1))

    group = lane_iota(rows) >> 4

    def pack_edges(kind):
        for part in range(2):
            planes = [l0.cb[kind, 0, 8 * part + j, own, :] for j in range(8)]
            for side in range(2):
                merged = planes[0] if side == 0 else pltpu.roll(planes[0], 16, 1)
                for j in range(1, 8):
                    shift = (16 * j + 16 * side) % LANES
                    moved = pltpu.roll(planes[j], shift, 1) if shift else planes[j]
                    merged = jnp.where(group == j, moved, merged)
                edges[kind, side, part] = merged

    load_phase.wait()
    phase = phase_ref[...]
    v0, v1, v2 = table_ref[0], table_ref[1], table_ref[2]
    l0.cb[0, 0, :, own, :] = 1.0 / jnp.where(phase == 0, v0, jnp.where(phase == 1, v1, v2))
    pack_edges(0)
    load_source.wait()
    pack_edges(1)

    has_lower = lax.div(c + n_cast - 1, n_cast)
    has_upper = lax.div(2 * n_cast - 2 - c, n_cast)
    pl.semaphore_wait(barrier, n_cast + n_span - 2 + 2 * has_lower + 2 * has_upper)

    def block_copy(kind, dc):
        block = 1 - dc
        return pltpu.make_async_remote_copy(
            src_ref=l0.cb.at[kind, 0, :, pl.ds(PAD + rows, rows), :],
            dst_ref=l0.cb.at[kind, 0, :, pl.ds(PAD + block * rows, rows), :],
            send_sem=send_sem.at[kind, 6 + (dc + 1) // 2],
            recv_sem=recv_sem.at[kind, 6 + (dc + 1) // 2],
            device_id=(c + dc, s),
            device_id_type=MESH,
        )

    def edge_copy(kind, dc, side):
        return pltpu.make_async_remote_copy(
            src_ref=edges.at[kind, side],
            dst_ref=halos.at[kind, side, :, pl.ds((1 - dc) * rows, rows), :],
            send_sem=send_sem.at[kind, 3 * side + dc + 1],
            recv_sem=recv_sem.at[kind, 3 * side + dc + 1],
            device_id=(c + dc, span_at(2 * side - 1)),
            device_id_type=MESH,
        )

    def toward(kind, dc):
        return [block_copy(kind, dc), edge_copy(kind, dc, 0), edge_copy(kind, dc, 1)]

    def send_halo(kind):
        @pl.when(c < n_cast - 1)
        def _():
            for copy in toward(kind, 1):
                copy.start()

        @pl.when(c > 0)
        def _():
            for copy in toward(kind, -1):
                copy.start()

        edge_copy(kind, 0, 0).start()
        edge_copy(kind, 0, 1).start()

    first_half = lane_iota(3 * rows) < 64

    def take_halo(kind):
        edge_copy(kind, 0, 0).wait()
        edge_copy(kind, 0, 1).wait()

        @pl.when(c > 0)
        def _():
            for copy in toward(kind, 1):
                copy.wait_recv()
            for copy in toward(kind, -1):
                copy.wait_send()

        @pl.when(c < n_cast - 1)
        def _():
            for copy in toward(kind, -1):
                copy.wait_recv()
            for copy in toward(kind, 1):
                copy.wait_send()

        for part in range(2):
            above, beneath = halos[kind, 0, part], halos[kind, 1, part]
            for j in range(8):
                a = pltpu.roll(above, (LANES - 16 * j) % LANES, 1) if j else above
                b = pltpu.roll(beneath, 112 - 16 * j, 1) if j < 7 else beneath
                l0.cb[kind, 1, 8 * part + j, PAD:PAD + 3 * rows, :] = jnp.where(first_half, a, b)

    key, lane = (lax.broadcasted_iota(jnp.int32, (LANES, LANES), d) for d in (0, 1))
    narrow = as_matrix((lane == (key >> 1)) & (key < 64))
    quarter = lane_iota(rows2) >> 5

    def pack_own(kind, ref, first, scale):
        for h in range(l2.height):
            small[h] = children(
                ref[plane, pl.ds(first + odd, rows2, stride=2), :]
                for plane in (2 * h, 2 * h + 1) for odd in range(2)
            ) * scale
        product = select_mm(small[...].reshape(rows2 * l2.height, LANES), narrow)
        product = product.reshape(l2.height, rows2, LANES)
        merged = product[0]
        for h in range(1, l2.height):
            merged = merged + pltpu.roll(product[h], 32 * h, 1)
        packed[kind] = merged
        gathered[kind, s, c] = merged

    def along_cast(kind):
        return [pltpu.make_async_remote_copy(
            src_ref=packed.at[kind], dst_ref=gathered.at[kind, s, c],
            send_sem=send_c.at[kind, d - 1], recv_sem=recv_c.at[kind, d - 1],
            device_id=(cast_at(d), s), device_id_type=MESH) for d in range(1, n_cast)]

    def along_span(kind):
        return [pltpu.make_async_remote_copy(
            src_ref=gathered.at[kind, s], dst_ref=gathered.at[kind, s],
            send_sem=send_s.at[kind, d - 1], recv_sem=recv_s.at[kind, d - 1],
            device_id=(c, span_at(d)), device_id_type=MESH) for d in range(1, n_span)]

    def start(copies):
        for copy in copies:
            copy.start()

    def finished(copies):
        for copy in copies:
            copy.wait()

    def unpack(kind):
        for t in range(l2.tiles):
            for cc in range(n_cast):
                blocks = [gathered[kind, 4 * t + j, cc] for j in range(4)]
                for h in range(l2.height):
                    joined = None
                    for j in range(4):
                        shift = (32 * (j - h)) % LANES
                        moved = pltpu.roll(blocks[j], shift, 1) if shift else blocks[j]
                        joined = moved if joined is None else jnp.where(quarter == j, moved, joined)
                    at = PAD + rows2 * cc
                    l2.cb[kind, t, h, at:at + rows2, :] = joined

    send_halo(0)
    send_halo(1)
    stacked = jnp.concatenate([
        children(
            l0.cb[0, 0, plane, pl.ds(PAD + rows + odd, rows1, stride=2), :]
            for plane in (2 * h, 2 * h + 1) for odd in range(2)
        ) * (0.125 * 0.25)
        for h in range(l1.height)
    ], axis=0)
    half[...] = select_mm(stacked, as_matrix(lane == (key >> 1))).reshape(l1.height, rows1, LANES)
    pack_own(0, half, 0, 0.125 * 0.25)
    start(along_cast(0))
    for level in levels:
        level.clear_pads()
        level.clear_coeff_pads()
    tall[...] = jnp.zeros(tall.shape, jnp.float32)
    finished(along_cast(0))
    start(along_span(0))

    take_halo(0)
    l0.prepare(rows * c - rows, rows * n_cast)
    coarsen(l0, l1, 0)
    l1.prepare(rows1 * c - rows1, rows1 * n_cast)

    take_halo(1)
    l0.begin()
    l0.relax(l0.xa, l0.xb, 0, 3 * rows)
    l0.keep_remainder(l0.xb, 0, 3 * rows)
    coarsen(l0, l1, 1)
    l1.begin()
    l1.relax(l1.xa, l1.xb, 0, 3 * rows1)
    l1.keep_remainder(l1.xb, rows1, rows1)
    pack_own(1, l1.rem.at[0], rows1, 0.125)

    start(along_cast(1))
    finished(along_span(0))
    unpack(0)
    finished(along_cast(1))
    start(along_span(1))
    l2.prepare(0, l2.rows)
    coarsen(l2, l3, 0)
    l3.prepare(0, l3.rows)
    finished(along_span(1))
    unpack(1)

    l2.begin()
    l2.relax(l2.xa, l2.xb, 0, l2.rows)
    l2.keep_remainder(l2.xb, 0, l2.rows)
    coarsen(l2, l3, 1)
    l3.begin()
    x, y = l3.xa, l3.xb
    for _ in range(COARSE - 1):
        l3.relax(x, y, 0, l3.rows)
        x, y = y, x
    refine_add(l3, x, l2, l2.xb, l2.xa, wide2)
    l2.relax(l2.xa, l2.xb, 0, l2.rows)
    l2.relax(l2.xb, l2.xa, 0, l2.rows)

    period = 64 * n_span
    place = jnp.where(lane < 96, lane, lane - LANES) + 64 * s
    place = jnp.where(place < 0, place + period, jnp.where(place >= period, place - period, place)) >> 1
    product = None
    for t in range(l2.tiles):
        stacked = l2.xa[t, 1:1 + l2.height, PAD:PAD + l2.rows, :].reshape(l2.height * l2.rows, LANES)
        term = select_mm(stacked, as_matrix(key + LANES * t == place))
        product = term if product is None else product + term
    product = product.reshape(l2.height, l2.rows, LANES)
    for h in range(l2.height):
        for odd in range(2):
            tall[h, pl.ds(PAD + odd, l2.rows, stride=2), :] = product[h]
    for h in range(l2.height):
        window = tall[h, pl.ds(pl.multiple_of(8 * c, 8), 3 * rows1), :]
        for plane in (2 * h, 2 * h + 1):
            l1.xa[0, plane + 1, PAD:PAD + 3 * rows1, :] = l1.xb[0, plane + 1, PAD:PAD + 3 * rows1, :] + window
    l1.relax(l1.xa, l1.xb, 0, 3 * rows1)
    l1.relax(l1.xb, l1.xa, 0, 3 * rows1)
    refine_add(l1, l1.xa, l0, l0.xb, l0.xa, wide0)
    l0.relax(l0.xa, l0.xb, rows - 8, rows + 16)
    l0.relax(l0.xb, l0.xa, rows - 8, rows + 16)

    def finish(t, h, value, centre):
        field_ref[h] = centre
        residual_ref[h] = value

    l0.remainder(l0.xa, rows, rows, 1, finish)


def solution(mesh):
    n_cast, n_span = mesh.shape["cast"], mesh.shape["span"]

    def shards(phase, viscosity_table, pressure_source):
        height, rows, width = phase.shape
        assert (height, rows, width) == (16, 16, LANES)
        levels = [
            Level(2, 16, 3 * rows, 4),
            Level(1, 8, 3 * rows // 2, 8),
            Level(n_span // 4, 4, 4 * n_cast, 4),
            Level(n_span // 8, 2, 2 * n_cast, 2),
        ]
        scratch = []
        for level in levels:
            scratch += level.scratch()
        dma = pltpu.SemaphoreType.DMA
        scratch += [
            pltpu.VMEM(phase.shape, jnp.int32),
            pltpu.VMEM((2, 2, 2, rows, LANES), jnp.float32),
            pltpu.VMEM((2, 2, 2, 3 * rows, LANES), jnp.float32),
            pltpu.VMEM((8, 8, LANES), jnp.float32),
            pltpu.VMEM((4, 4, LANES), jnp.float32),
            pltpu.VMEM((2, 4, LANES), jnp.float32),
            pltpu.VMEM((2, n_span, n_cast, 4, LANES), jnp.float32),
            pltpu.VMEM((4, 8 * n_cast + 2 * PAD, LANES), jnp.float32),
            pltpu.VMEM((8, 3 * rows, LANES), jnp.float32),
            pltpu.VMEM((2, 4 * n_cast, LANES), jnp.float32),
            dma((2,)),
            dma((2, 8)), dma((2, 8)),
            dma((2, n_cast - 1)), dma((2, n_cast - 1)),
            dma((2, n_span - 1)), dma((2, n_span - 1)),
        ]
        block = jax.ShapeDtypeStruct(phase.shape, jnp.float32)
        vmem = pl.BlockSpec(memory_space=pltpu.VMEM)
        anywhere = pl.BlockSpec(memory_space=pl.ANY)
        return pl.pallas_call(
            functools.partial(kernel, n_cast, n_span, levels),
            out_shape=(block, block),
            in_specs=[pl.BlockSpec(memory_space=pltpu.SMEM), anywhere, anywhere],
            out_specs=(vmem, vmem),
            scratch_shapes=scratch,
            compiler_params=pltpu.CompilerParams(
                collective_id=0, has_side_effects=True, vmem_limit_bytes=48 * 2**20
            ),
        )(viscosity_table, phase, pressure_source)

    placed = P(None, "cast", "span")
    return jax.shard_map(
        shards, mesh=mesh, in_specs=(placed, P(), placed), out_specs=(placed, placed), check_vma=False
    )
```

```python
import functools
import jax
import jax.numpy as jnp
from jax import lax
from jax.experimental import pallas as pl
from jax.experimental.pallas import tpu as pltpu
from jax.sharding import PartitionSpec as P

LEVELS = 3
PRE = 2
POST = 2
COARSE = 8
PAD = 8
LANES = 128

relax_weight = 0.8
MESH = pl.DeviceIdType.MESH


def inverse(a):
    r = pl.reciprocal(a, approx=True)
    r = r * (2.0 - a * r)
    return r * (2.0 - a * r)


def harmonic(a, b):
    return 2.0 * a * b * inverse(a + b)


def lane_iota(rows):
    return lax.broadcasted_iota(jnp.int32, (rows, LANES), 1)


def from_lower(tiles):
    rolled = [pltpu.roll(v, 1, 1) for v in tiles]
    if len(tiles) == 1:
        return rolled
    edge = lane_iota(tiles[0].shape[0]) == 0
    return [jnp.where(edge, rolled[t - 1], rolled[t]) for t in range(len(tiles))]


def from_upper(tiles):
    rolled = [pltpu.roll(v, LANES - 1, 1) for v in tiles]
    if len(tiles) == 1:
        return rolled
    edge = lane_iota(tiles[0].shape[0]) == LANES - 1
    n = len(tiles)
    return [jnp.where(edge, rolled[(t + 1) % n], rolled[t]) for t in range(n)]


def select_mm(values, matrix):
    high = values.astype(jnp.bfloat16)
    low = (values - high.astype(jnp.float32)).astype(jnp.bfloat16)
    return jnp.dot(high, matrix, preferred_element_type=jnp.float32) + jnp.dot(
        low, matrix, preferred_element_type=jnp.float32
    )


def as_matrix(mask):
    return jnp.where(mask, 1.0, 0.0).astype(jnp.bfloat16)


class Level:
    def __init__(self, tiles, height, rows, unroll):
        self.tiles, self.height, self.rows, self.unroll = tiles, height, rows, unroll

    def scratch(self):
        t, h, r = self.tiles, self.height, self.rows
        grown = r + 2 * PAD
        field = pltpu.VMEM((t, h, r, LANES), jnp.float32)
        return [
            pltpu.VMEM((2, t, h, grown, LANES), jnp.float32),
            pltpu.VMEM((t, h + 2, grown, LANES), jnp.float32),
            pltpu.VMEM((t, h + 2, grown, LANES), jnp.float32),
            pltpu.VMEM((t, h, r + PAD, LANES), jnp.float32),
            field, field,
            pltpu.VMEM((t, h + 1, r, LANES), jnp.float32),
            field, field,
            field,
        ]

    def bind(self, refs):
        (self.cb, self.xa, self.xb, self.cl, self.sl, self.su, self.fh,
         self.diag, self.weight, self.rem) = refs

    def loop(self, body, after=None):
        def step(i, carry):
            for k in range(self.unroll):
                body(i * self.unroll + k, k)
            if after is not None:
                after(i)
            return carry
        if self.unroll == self.height:
            step(0, 0)
        else:
            lax.fori_loop(0, self.height // self.unroll, step, 0)

    def clear_pads(self):
        t, h, r = self.tiles, self.height, self.rows
        for x in (self.xa, self.xb):
            x[:, :, 0:PAD, :] = jnp.zeros((t, h + 2, PAD, LANES), jnp.float32)
            x[:, :, PAD + r:, :] = jnp.zeros((t, h + 2, PAD, LANES), jnp.float32)
            x[:, 0:1, PAD:PAD + r, :] = jnp.zeros((t, 1, r, LANES), jnp.float32)
            x[:, h + 1:h + 2, PAD:PAD + r, :] = jnp.zeros((t, 1, r, LANES), jnp.float32)
        self.cl[:, :, r:, :] = jnp.zeros((t, h, PAD, LANES), jnp.float32)
        self.fh[:, 0:1] = jnp.zeros((t, 1, r, LANES), jnp.float32)

    def clear_coeff_pads(self):
        t, h, r = self.tiles, self.height, self.rows
        self.cb[0, :, :, 0:PAD, :] = jnp.ones((t, h, PAD, LANES), jnp.float32)
        self.cb[0, :, :, PAD + r:, :] = jnp.ones((t, h, PAD, LANES), jnp.float32)

    def prepare(self, first_row, total_rows):
        t_n, h_n, r = self.tiles, self.height, self.rows
        place = lax.broadcasted_iota(jnp.int32, (r, LANES), 0) + first_row
        at_start = place == 0
        at_stop = place == total_rows - 1
        at_wall = at_start | (place == total_rows)
        held = {}

        def body(h, k):
            coeff = [self.cb[0, t, h, PAD:PAD + r, :] for t in range(t_n)]
            span_lower = [harmonic(a, b) for a, b in zip(from_lower(coeff), coeff)]
            span_upper = from_upper(span_lower)
            top = min(h + 1, h_n - 1) if self.unroll == h_n else jnp.minimum(h + 1, h_n - 1)
            for t in range(t_n):
                c = coeff[t]
                lower = harmonic(self.cb[0, t, h, PAD - 1:PAD - 1 + r, :], c)
                lower = jnp.where(at_wall, 0.0, lower)
                self.cl[t, h, 0:r, :] = lower
                upper = self.cl[t, h, 1:1 + r, :]
                lower = jnp.where(at_start, c, lower)
                upper = jnp.where(at_stop, c, upper)
                self.sl[t, h] = span_lower[t]
                self.su[t, h] = span_upper[t]
                height_upper = harmonic(c, self.cb[0, t, top, PAD:PAD + r, :])
                height_upper = jnp.where(h < h_n - 1, height_upper, 0.0)
                height_lower = held[t] if k else self.fh[t, h]
                held[t] = height_upper
                self.fh[t, h + 1] = height_upper
                diagonal = (lower + upper + span_lower[t] + span_upper[t]
                            + height_lower + height_upper)
                self.diag[t, h] = diagonal
                self.weight[t, h] = relax_weight * inverse(diagonal)
        self.loop(body)

    def begin(self):
        r = self.rows

        def body(h, k):
            for t in range(self.tiles):
                self.xa[t, h + 1, PAD:PAD + r, :] = self.weight[t, h] * self.cb[1, t, h, PAD:PAD + r, :]
        self.loop(body)

    def near(self, x, h, start, n, tiles):
        centre = [x[t, h + 1, pl.ds(PAD + start, n), :] for t in range(self.tiles)]
        lower, upper = from_lower(centre), from_upper(centre)
        rows = pl.ds(start, n)
        out = []
        for t in range(tiles):
            out.append(
                self.cl[t, h, rows, :] * x[t, h + 1, pl.ds(PAD - 1 + start, n), :]
                + self.cl[t, h, pl.ds(start + 1, n), :] * x[t, h + 1, pl.ds(PAD + 1 + start, n), :]
                + self.sl[t, h, rows, :] * lower[t]
                + self.su[t, h, rows, :] * upper[t]
                + self.fh[t, h, rows, :] * x[t, h, pl.ds(PAD + start, n), :]
                + self.fh[t, h + 1, rows, :] * x[t, h + 2, pl.ds(PAD + start, n), :]
                + self.cb[1, t, h, pl.ds(PAD + start, n), :]
            )
        return centre, out

    def relax(self, x, y, start, n):
        def body(h, k):
            centre, near = self.near(x, h, start, n, self.tiles)
            for t in range(self.tiles):
                y[t, h + 1, pl.ds(PAD + start, n), :] = (
                    (1.0 - relax_weight) * centre[t] + self.weight[t, h, pl.ds(start, n), :] * near[t]
                )
        self.loop(body)

    def relax_held(self, sweeps):
        t_n, h_n, r = self.tiles, self.height, self.rows
        at = slice(PAD, PAD + r)
        cells = [(t, h) for h in range(h_n) for t in range(t_n)]
        weight = {k: self.weight[k[0], k[1]] for k in cells}
        base = {k: weight[k] * self.cb[1, k[0], k[1], at, :] for k in cells}
        cast_lower = {k: weight[k] * self.cl[k[0], k[1], 0:r, :] for k in cells}
        cast_upper = {k: weight[k] * self.cl[k[0], k[1], 1:1 + r, :] for k in cells}
        span_lower = {k: weight[k] * self.sl[k[0], k[1]] for k in cells}
        span_upper = {k: weight[k] * self.su[k[0], k[1]] for k in cells}
        height_lower = {k: weight[k] * self.fh[k[0], k[1]] for k in cells}
        height_upper = {k: weight[k] * self.fh[k[0], k[1] + 1] for k in cells}
        x = base
        for _ in range(sweeps - 1):
            new = {}
            for h in range(h_n):
                plane = [x[t, h] for t in range(t_n)]
                lower, upper = from_lower(plane), from_upper(plane)
                for t in range(t_n):
                    k = (t, h)
                    local = (1.0 - relax_weight) * x[k] + base[k]
                    if h > 0:
                        local = local + height_lower[k] * x[t, h - 1]
                    if h < h_n - 1:
                        local = local + height_upper[k] * x[t, h + 1]
                    cast = (cast_lower[k] * pltpu.roll(x[k], 1, 0)
                            + cast_upper[k] * pltpu.roll(x[k], r - 1, 0))
                    new[k] = local + cast + (span_lower[k] * lower[t] + span_upper[k] * upper[t])
            x = new
        for t, h in cells:
            self.xa[t, h + 1, at, :] = x[t, h]

    def remainder(self, x, start, n, tiles, store, after=None):
        def body(h, k):
            centre, near = self.near(x, h, start, n, tiles)
            for t in range(tiles):
                store(t, h, near[t] - self.diag[t, h, pl.ds(start, n), :] * centre[t])
        self.loop(body, after)

    def keep_remainder(self, x, start, n):
        def store(t, h, value):
            self.rem[t, h, pl.ds(start, n), :] = value
        self.remainder(x, start, n, self.tiles, store)


def children(pieces):
    total = None
    for piece in pieces:
        total = piece if total is None else total + piece
    return total


def coarsen(fine, coarse, kind):
    half = fine.rows // 2
    key, lane = (lax.broadcasted_iota(jnp.int32, (LANES, LANES), d) for d in (0, 1))
    into = [as_matrix(lane == (key >> 1)), as_matrix(lane == 64 + (key >> 1))]
    ref, first = (fine.cb.at[0], PAD) if kind == 0 else (fine.rem, 0)
    scale = 0.125 * 0.25 if kind == 0 else 0.125
    for t in range(coarse.tiles):
        total = None
        for side in range(2):
            parts = [
                children(
                    ref[2 * t + side, plane, pl.ds(first + odd, half, stride=2), :]
                    for plane in (2 * h, 2 * h + 1) for odd in range(2)
                ) * scale
                for h in range(coarse.height)
            ]
            product = select_mm(jnp.concatenate(parts, axis=0), into[side])
            total = product if total is None else total + product
        coarse.cb[kind, t, :, PAD:PAD + half, :] = total.reshape(coarse.height, half, LANES)


def refine_add(coarse, x, fine, y, z, wide, start, n):
    half, first = n // 2, start // 2
    key, lane = (lax.broadcasted_iota(jnp.int32, (LANES, LANES), d) for d in (0, 1))
    out_of = [as_matrix(key == (lane >> 1)), as_matrix(key == 64 + (lane >> 1))]
    for t in range(coarse.tiles):
        stacked = x[t, 1:1 + coarse.height, PAD + first:PAD + first + half, :].reshape(coarse.height * half, LANES)
        for side in range(2):
            f = 2 * t + side
            product = select_mm(stacked, out_of[side]).reshape(coarse.height, half, LANES)
            for h in range(coarse.height):
                for odd in range(2):
                    wide[h, pl.ds(odd, half, stride=2), :] = product[h]
            for h in range(coarse.height):
                rows = wide[h, 0:n, :]
                for plane in (2 * h, 2 * h + 1):
                    at = pl.ds(PAD + start, n)
                    z[f, plane + 1, at, :] = y[f, plane + 1, at, :] + rows


def kernel(n_cast, n_span, levels, table_hbm, phase_hbm, source_hbm, field_hbm, residual_hbm, *scratch):
    for i, level in enumerate(levels):
        level.bind(scratch[10 * i:10 * i + 10])
    l0, l1, l2, l3 = levels
    (table_ref, phase_ref, edges, halos, half, small, packed, gathered, tall, wide0, wide2, load_sem, save_sem,
     send_sem, recv_sem, send_c, recv_c, send_s, recv_s) = scratch[40:]
    c, s = lax.axis_index("cast"), lax.axis_index("span")
    height, rows, _ = phase_ref.shape
    rows1, rows2 = rows // 2, rows // 4
    own = slice(PAD + rows, PAD + 2 * rows)
    load_phase = pltpu.make_async_copy(phase_hbm, phase_ref, load_sem.at[0])
    load_source = pltpu.make_async_copy(source_hbm, l0.cb.at[1, 0, :, own, :], load_sem.at[1])
    load_table = pltpu.make_async_copy(table_hbm, table_ref, load_sem.at[2])
    load_table.start()
    load_phase.start()
    load_source.start()

    def span_at(offset):
        return lax.rem(s + offset + n_span, n_span)

    def cast_at(offset):
        return lax.rem(c + offset + n_cast, n_cast)

    def blank(block):
        at = slice(PAD + block * rows, PAD + (block + 1) * rows)
        l0.cb[0, 0, :, at, :] = jnp.ones((height, rows, LANES), jnp.float32)
        l0.cb[1, 0, :, at, :] = jnp.zeros((height, rows, LANES), jnp.float32)
        within = slice(block * rows, (block + 1) * rows)
        for side in range(2):
            halos[0, side, :, within, :] = jnp.ones((2, rows, LANES), jnp.float32)
            halos[1, side, :, within, :] = jnp.zeros((2, rows, LANES), jnp.float32)

    @pl.when(c == 0)
    def _():
        blank(0)

    @pl.when(c == n_cast - 1)
    def _():
        blank(2)

    barrier = pltpu.get_barrier_semaphore()

    def greet(cast, span):
        pl.semaphore_signal(barrier, inc=1, device_id=(cast, span), device_id_type=MESH)

    for d in range(1, n_cast):
        greet(cast_at(d), s)
    for d in range(1, n_span):
        greet(c, span_at(d))

    @pl.when(c > 0)
    def _():
        greet(c - 1, span_at(1))
        greet(c - 1, span_at(-1))

    @pl.when(c < n_cast - 1)
    def _():
        greet(c + 1, span_at(1))
        greet(c + 1, span_at(-1))

    group = lane_iota(rows) >> 4

    def pack_edges(kind):
        for part in range(2):
            planes = [l0.cb[kind, 0, 8 * part + j, own, :] for j in range(8)]
            for side in range(2):
                merged = planes[0] if side == 0 else pltpu.roll(planes[0], 16, 1)
                for j in range(1, 8):
                    shift = (16 * j + 16 * side) % LANES
                    moved = pltpu.roll(planes[j], shift, 1) if shift else planes[j]
                    merged = jnp.where(group == j, moved, merged)
                edges[kind, side, part] = merged

    load_table.wait()
    load_phase.wait()
    phase = phase_ref[...]
    v0, v1, v2 = table_ref[0], table_ref[1], table_ref[2]
    l0.cb[0, 0, :, own, :] = 1.0 / jnp.where(phase == 0, v0, jnp.where(phase == 1, v1, v2))
    pack_edges(0)
    load_source.wait()
    pack_edges(1)

    has_lower = lax.div(c + n_cast - 1, n_cast)
    has_upper = lax.div(2 * n_cast - 2 - c, n_cast)
    pl.semaphore_wait(barrier, n_cast + n_span - 2 + 2 * has_lower + 2 * has_upper)

    def block_copy(kind, dc):
        block = 1 - dc
        return pltpu.make_async_remote_copy(
            src_ref=l0.cb.at[kind, 0, :, pl.ds(PAD + rows, rows), :],
            dst_ref=l0.cb.at[kind, 0, :, pl.ds(PAD + block * rows, rows), :],
            send_sem=send_sem.at[kind, 6 + (dc + 1) // 2],
            recv_sem=recv_sem.at[kind, 6 + (dc + 1) // 2],
            device_id=(c + dc, s),
            device_id_type=MESH,
        )

    def edge_copy(kind, dc, side):
        return pltpu.make_async_remote_copy(
            src_ref=edges.at[kind, side],
            dst_ref=halos.at[kind, side, :, pl.ds((1 - dc) * rows, rows), :],
            send_sem=send_sem.at[kind, 3 * side + dc + 1],
            recv_sem=recv_sem.at[kind, 3 * side + dc + 1],
            device_id=(c + dc, span_at(2 * side - 1)),
            device_id_type=MESH,
        )

    def toward(kind, dc):
        return [block_copy(kind, dc), edge_copy(kind, dc, 0), edge_copy(kind, dc, 1)]

    def send_halo(kind):
        @pl.when(c < n_cast - 1)
        def _():
            for copy in toward(kind, 1):
                copy.start()

        @pl.when(c > 0)
        def _():
            for copy in toward(kind, -1):
                copy.start()

        edge_copy(kind, 0, 0).start()
        edge_copy(kind, 0, 1).start()

    first_half = lane_iota(3 * rows) < 64

    def take_halo(kind):
        edge_copy(kind, 0, 0).wait()
        edge_copy(kind, 0, 1).wait()

        @pl.when(c > 0)
        def _():
            for copy in toward(kind, 1):
                copy.wait_recv()
            for copy in toward(kind, -1):
                copy.wait_send()

        @pl.when(c < n_cast - 1)
        def _():
            for copy in toward(kind, -1):
                copy.wait_recv()
            for copy in toward(kind, 1):
                copy.wait_send()

        for part in range(2):
            above, beneath = halos[kind, 0, part], halos[kind, 1, part]
            for j in range(8):
                a = pltpu.roll(above, (LANES - 16 * j) % LANES, 1) if j else above
                b = pltpu.roll(beneath, 112 - 16 * j, 1) if j < 7 else beneath
                l0.cb[kind, 1, 8 * part + j, PAD:PAD + 3 * rows, :] = jnp.where(first_half, a, b)

    key, lane = (lax.broadcasted_iota(jnp.int32, (LANES, LANES), d) for d in (0, 1))
    narrow = as_matrix((lane == (key >> 1)) & (key < 64))
    quarter = lane_iota(rows2) >> 5

    def pack_own(kind, ref, first, scale):
        for h in range(l2.height):
            small[h] = children(
                ref[plane, pl.ds(first + odd, rows2, stride=2), :]
                for plane in (2 * h, 2 * h + 1) for odd in range(2)
            ) * scale
        product = select_mm(small[...].reshape(rows2 * l2.height, LANES), narrow)
        product = product.reshape(l2.height, rows2, LANES)
        merged = product[0]
        for h in range(1, l2.height):
            merged = merged + pltpu.roll(product[h], 32 * h, 1)
        packed[kind] = merged
        gathered[kind, s, c] = merged

    def along_cast(kind):
        return [pltpu.make_async_remote_copy(
            src_ref=packed.at[kind], dst_ref=gathered.at[kind, s, c],
            send_sem=send_c.at[kind, d - 1], recv_sem=recv_c.at[kind, d - 1],
            device_id=(cast_at(d), s), device_id_type=MESH) for d in range(1, n_cast)]

    def along_span(kind):
        return [pltpu.make_async_remote_copy(
            src_ref=gathered.at[kind, s], dst_ref=gathered.at[kind, s],
            send_sem=send_s.at[kind, d - 1], recv_sem=recv_s.at[kind, d - 1],
            device_id=(c, span_at(d)), device_id_type=MESH) for d in range(1, n_span)]

    def start(copies):
        for copy in copies:
            copy.start()

    def finished(copies):
        for copy in copies:
            copy.wait()

    def unpack(kind):
        for t in range(l2.tiles):
            for cc in range(n_cast):
                blocks = [gathered[kind, 4 * t + j, cc] for j in range(4)]
                for h in range(l2.height):
                    joined = None
                    for j in range(4):
                        shift = (32 * (j - h)) % LANES
                        moved = pltpu.roll(blocks[j], shift, 1) if shift else blocks[j]
                        joined = moved if joined is None else jnp.where(quarter == j, moved, joined)
                    at = PAD + rows2 * cc
                    l2.cb[kind, t, h, at:at + rows2, :] = joined

    send_halo(0)
    send_halo(1)
    stacked = jnp.concatenate([
        children(
            l0.cb[0, 0, plane, pl.ds(PAD + rows + odd, rows1, stride=2), :]
            for plane in (2 * h, 2 * h + 1) for odd in range(2)
        ) * (0.125 * 0.25)
        for h in range(l1.height)
    ], axis=0)
    half[...] = select_mm(stacked, as_matrix(lane == (key >> 1))).reshape(l1.height, rows1, LANES)
    pack_own(0, half, 0, 0.125 * 0.25)
    start(along_cast(0))
    for level in levels:
        level.clear_pads()
        level.clear_coeff_pads()
    tall[...] = jnp.zeros(tall.shape, jnp.float32)
    finished(along_cast(0))
    start(along_span(0))

    take_halo(0)
    l0.prepare(rows * c - rows, rows * n_cast)
    coarsen(l0, l1, 0)
    l1.prepare(rows1 * c - rows1, rows1 * n_cast)

    take_halo(1)
    l0.begin()
    l0.relax(l0.xa, l0.xb, 0, 3 * rows)
    l0.keep_remainder(l0.xb, 0, 3 * rows)
    coarsen(l0, l1, 1)
    l1.begin()
    l1.relax(l1.xa, l1.xb, 0, 3 * rows1)
    l1.keep_remainder(l1.xb, rows1, rows1)
    pack_own(1, l1.rem.at[0], rows1, 0.125)

    start(along_cast(1))
    finished(along_span(0))
    unpack(0)
    finished(along_cast(1))
    start(along_span(1))
    l2.prepare(0, l2.rows)
    coarsen(l2, l3, 0)
    l3.prepare(0, l3.rows)
    finished(along_span(1))
    unpack(1)

    l2.begin()
    l2.relax(l2.xa, l2.xb, 0, l2.rows)
    l2.keep_remainder(l2.xb, 0, l2.rows)
    coarsen(l2, l3, 1)
    l3.relax_held(COARSE)
    refine_add(l3, l3.xa, l2, l2.xb, l2.xa, wide2, 0, l2.rows)
    l2.relax(l2.xa, l2.xb, 0, l2.rows)
    l2.relax(l2.xb, l2.xa, 0, l2.rows)

    period = 64 * n_span
    place = jnp.where(lane < 96, lane, lane - LANES) + 64 * s
    place = jnp.where(place < 0, place + period, jnp.where(place >= period, place - period, place)) >> 1
    product = None
    for t in range(l2.tiles):
        stacked = l2.xa[t, 1:1 + l2.height, PAD:PAD + l2.rows, :].reshape(l2.height * l2.rows, LANES)
        term = select_mm(stacked, as_matrix(key + LANES * t == place))
        product = term if product is None else product + term
    product = product.reshape(l2.height, l2.rows, LANES)
    for h in range(l2.height):
        for odd in range(2):
            tall[h, pl.ds(PAD + odd, l2.rows, stride=2), :] = product[h]
    for h in range(l2.height):
        window = tall[h, pl.ds(pl.multiple_of(8 * c, 8), 3 * rows1), :]
        for plane in (2 * h, 2 * h + 1):
            l1.xa[0, plane + 1, PAD:PAD + 3 * rows1, :] = l1.xb[0, plane + 1, PAD:PAD + 3 * rows1, :] + window
    l1.relax(l1.xa, l1.xb, 0, 3 * rows1)
    l1.relax(l1.xb, l1.xa, 0, 3 * rows1)
    refine_add(l1, l1.xa, l0, l0.xb, l0.xa, wide0, rows - 8, rows + 16)
    l0.relax(l0.xa, l0.xb, rows - 8, rows + 16)
    l0.relax(l0.xb, l0.xa, rows - 8, rows + 16)

    save_field = pltpu.make_async_copy(
        l0.xa.at[0, pl.ds(1, height), pl.ds(PAD + rows, rows), :], field_hbm, load_sem.at[0])
    save_field.start()

    def save_group(i):
        planes = pl.ds(i * l0.unroll, l0.unroll)
        return pltpu.make_async_copy(
            l0.rem.at[0, planes, pl.ds(rows, rows), :], residual_hbm.at[planes], save_sem.at[i])

    def finish(t, h, value):
        l0.rem[t, h, rows:2 * rows, :] = value

    l0.remainder(l0.xa, rows, rows, 1, finish, lambda i: save_group(i).start())
    save_field.wait()
    for i in range(height // l0.unroll):
        save_group(i).wait()


def solution(mesh):
    n_cast, n_span = mesh.shape["cast"], mesh.shape["span"]

    def shards(phase, viscosity_table, pressure_source):
        height, rows, width = phase.shape
        assert (height, rows, width) == (16, 16, LANES)
        levels = [
            Level(2, 16, 3 * rows, 4),
            Level(1, 8, 3 * rows // 2, 8),
            Level(n_span // 4, 4, 4 * n_cast, 4),
            Level(n_span // 8, 2, 2 * n_cast, 2),
        ]
        scratch = []
        for level in levels:
            scratch += level.scratch()
        dma = pltpu.SemaphoreType.DMA
        scratch += [
            pltpu.SMEM((3,), jnp.float32),
            pltpu.VMEM(phase.shape, jnp.int32),
            pltpu.VMEM((2, 2, 2, rows, LANES), jnp.float32),
            pltpu.VMEM((2, 2, 2, 3 * rows, LANES), jnp.float32),
            pltpu.VMEM((8, 8, LANES), jnp.float32),
            pltpu.VMEM((4, 4, LANES), jnp.float32),
            pltpu.VMEM((2, 4, LANES), jnp.float32),
            pltpu.VMEM((2, n_span, n_cast, 4, LANES), jnp.float32),
            pltpu.VMEM((4, 8 * n_cast + 2 * PAD, LANES), jnp.float32),
            pltpu.VMEM((8, 3 * rows, LANES), jnp.float32),
            pltpu.VMEM((2, 4 * n_cast, LANES), jnp.float32),
            dma((3,)), dma((4,)),
            dma((2, 8)), dma((2, 8)),
            dma((2, n_cast - 1)), dma((2, n_cast - 1)),
            dma((2, n_span - 1)), dma((2, n_span - 1)),
        ]
        block = jax.ShapeDtypeStruct(phase.shape, jnp.float32)
        anywhere = pl.BlockSpec(memory_space=pltpu.HBM)
        return pl.pallas_call(
            functools.partial(kernel, n_cast, n_span, levels),
            out_shape=(block, block),
            in_specs=[anywhere, anywhere, anywhere],
            out_specs=(anywhere, anywhere),
            scratch_shapes=scratch,
            compiler_params=pltpu.CompilerParams(
                collective_id=0, has_side_effects=True, vmem_limit_bytes=63 * 2**20
            ),
        )(viscosity_table, phase, pressure_source)

    placed = P(None, "cast", "span")
    return jax.shard_map(
        shards, mesh=mesh, in_specs=(placed, P(), placed), out_specs=(placed, placed), check_vma=False
    )
```

```python
import functools
import jax
import jax.numpy as jnp
from jax import lax
from jax.experimental import pallas as pl
from jax.experimental.pallas import tpu as pltpu
from jax.sharding import PartitionSpec as P

LEVELS = 3
PRE = 2
POST = 2
COARSE = 8
PAD = 8
LANES = 128

relax_weight = 0.8
MESH = pl.DeviceIdType.MESH


def inverse(a):
    r = pl.reciprocal(a, approx=True)
    r = r * (2.0 - a * r)
    return r * (2.0 - a * r)


def harmonic(a, b):
    return 2.0 * a * b * inverse(a + b)


def lane_iota(rows):
    return lax.broadcasted_iota(jnp.int32, (rows, LANES), 1)


def from_lower(tiles):
    rolled = [pltpu.roll(v, 1, 1) for v in tiles]
    if len(tiles) == 1:
        return rolled
    edge = lane_iota(tiles[0].shape[0]) == 0
    return [jnp.where(edge, rolled[t - 1], rolled[t]) for t in range(len(tiles))]


def from_upper(tiles):
    rolled = [pltpu.roll(v, LANES - 1, 1) for v in tiles]
    if len(tiles) == 1:
        return rolled
    edge = lane_iota(tiles[0].shape[0]) == LANES - 1
    n = len(tiles)
    return [jnp.where(edge, rolled[(t + 1) % n], rolled[t]) for t in range(n)]


def select_mm(values, matrix):
    high = values.astype(jnp.bfloat16)
    low = (values - high.astype(jnp.float32)).astype(jnp.bfloat16)
    return jnp.dot(high, matrix, preferred_element_type=jnp.float32) + jnp.dot(
        low, matrix, preferred_element_type=jnp.float32
    )


def as_matrix(mask):
    return jnp.where(mask, 1.0, 0.0).astype(jnp.bfloat16)


class Level:
    def __init__(self, tiles, height, rows, unroll):
        self.tiles, self.height, self.rows, self.unroll = tiles, height, rows, unroll

    def scratch(self):
        t, h, r = self.tiles, self.height, self.rows
        grown = r + 2 * PAD
        field = pltpu.VMEM((t, h, r, LANES), jnp.float32)
        return [
            pltpu.VMEM((2, t, h, grown, LANES), jnp.float32),
            pltpu.VMEM((t, h + 2, grown, LANES), jnp.float32),
            pltpu.VMEM((t, h + 2, grown, LANES), jnp.float32),
            pltpu.VMEM((t, h, r + PAD, LANES), jnp.float32),
            field, field,
            pltpu.VMEM((t, h + 1, r, LANES), jnp.float32),
            field, field,
            field,
        ]

    def bind(self, refs):
        (self.cb, self.xa, self.xb, self.cl, self.sl, self.su, self.fh,
         self.diag, self.weight, self.rem) = refs

    def loop(self, body, after=None):
        def step(i, carry):
            for k in range(self.unroll):
                body(i * self.unroll + k, k)
            if after is not None:
                after(i)
            return carry
        if self.unroll == self.height:
            step(0, 0)
        else:
            lax.fori_loop(0, self.height // self.unroll, step, 0)

    def clear_pads(self):
        t, h, r = self.tiles, self.height, self.rows
        for x in (self.xa, self.xb):
            x[:, :, 0:PAD, :] = jnp.zeros((t, h + 2, PAD, LANES), jnp.float32)
            x[:, :, PAD + r:, :] = jnp.zeros((t, h + 2, PAD, LANES), jnp.float32)
            x[:, 0:1, PAD:PAD + r, :] = jnp.zeros((t, 1, r, LANES), jnp.float32)
            x[:, h + 1:h + 2, PAD:PAD + r, :] = jnp.zeros((t, 1, r, LANES), jnp.float32)
        self.cl[:, :, r:, :] = jnp.zeros((t, h, PAD, LANES), jnp.float32)
        self.fh[:, 0:1] = jnp.zeros((t, 1, r, LANES), jnp.float32)

    def clear_coeff_pads(self):
        t, h, r = self.tiles, self.height, self.rows
        self.cb[0, :, :, 0:PAD, :] = jnp.ones((t, h, PAD, LANES), jnp.float32)
        self.cb[0, :, :, PAD + r:, :] = jnp.ones((t, h, PAD, LANES), jnp.float32)

    def prepare(self, first_row, total_rows):
        t_n, h_n, r = self.tiles, self.height, self.rows
        place = lax.broadcasted_iota(jnp.int32, (r, LANES), 0) + first_row
        at_start = place == 0
        at_stop = place == total_rows - 1
        at_wall = at_start | (place == total_rows)
        held = {}

        def body(h, k):
            coeff = [self.cb[0, t, h, PAD:PAD + r, :] for t in range(t_n)]
            span_lower = [harmonic(a, b) for a, b in zip(from_lower(coeff), coeff)]
            span_upper = from_upper(span_lower)
            top = min(h + 1, h_n - 1) if self.unroll == h_n else jnp.minimum(h + 1, h_n - 1)
            for t in range(t_n):
                c = coeff[t]
                lower = harmonic(self.cb[0, t, h, PAD - 1:PAD - 1 + r, :], c)
                lower = jnp.where(at_wall, 0.0, lower)
                self.cl[t, h, 0:r, :] = lower
                upper = self.cl[t, h, 1:1 + r, :]
                lower = jnp.where(at_start, c, lower)
                upper = jnp.where(at_stop, c, upper)
                self.sl[t, h] = span_lower[t]
                self.su[t, h] = span_upper[t]
                height_upper = harmonic(c, self.cb[0, t, top, PAD:PAD + r, :])
                height_upper = jnp.where(h < h_n - 1, height_upper, 0.0)
                height_lower = held[t] if k else self.fh[t, h]
                held[t] = height_upper
                self.fh[t, h + 1] = height_upper
                diagonal = (lower + upper + span_lower[t] + span_upper[t]
                            + height_lower + height_upper)
                self.diag[t, h] = diagonal
                self.weight[t, h] = relax_weight * inverse(diagonal)
        self.loop(body)

    def begin(self):
        r = self.rows

        def body(h, k):
            for t in range(self.tiles):
                self.xa[t, h + 1, PAD:PAD + r, :] = self.weight[t, h] * self.cb[1, t, h, PAD:PAD + r, :]
        self.loop(body)

    def near(self, x, h, start, n, tiles):
        centre = [x[t, h + 1, pl.ds(PAD + start, n), :] for t in range(self.tiles)]
        lower, upper = from_lower(centre), from_upper(centre)
        rows = pl.ds(start, n)
        out = []
        for t in range(tiles):
            out.append(
                self.cl[t, h, rows, :] * x[t, h + 1, pl.ds(PAD - 1 + start, n), :]
                + self.cl[t, h, pl.ds(start + 1, n), :] * x[t, h + 1, pl.ds(PAD + 1 + start, n), :]
                + self.sl[t, h, rows, :] * lower[t]
                + self.su[t, h, rows, :] * upper[t]
                + self.fh[t, h, rows, :] * x[t, h, pl.ds(PAD + start, n), :]
                + self.fh[t, h + 1, rows, :] * x[t, h + 2, pl.ds(PAD + start, n), :]
                + self.cb[1, t, h, pl.ds(PAD + start, n), :]
            )
        return centre, out

    def relax(self, x, y, start, n):
        def body(h, k):
            centre, near = self.near(x, h, start, n, self.tiles)
            for t in range(self.tiles):
                y[t, h + 1, pl.ds(PAD + start, n), :] = (
                    (1.0 - relax_weight) * centre[t] + self.weight[t, h, pl.ds(start, n), :] * near[t]
                )
        self.loop(body)

    def relax_held(self, sweeps):
        t_n, h_n, r = self.tiles, self.height, self.rows
        at = slice(PAD, PAD + r)
        cells = [(t, h) for h in range(h_n) for t in range(t_n)]
        weight = {k: self.weight[k[0], k[1]] for k in cells}
        base = {k: weight[k] * self.cb[1, k[0], k[1], at, :] for k in cells}
        cast_lower = {k: weight[k] * self.cl[k[0], k[1], 0:r, :] for k in cells}
        cast_upper = {k: weight[k] * self.cl[k[0], k[1], 1:1 + r, :] for k in cells}
        span_lower = {k: weight[k] * self.sl[k[0], k[1]] for k in cells}
        span_upper = {k: weight[k] * self.su[k[0], k[1]] for k in cells}
        height_lower = {k: weight[k] * self.fh[k[0], k[1]] for k in cells}
        height_upper = {k: weight[k] * self.fh[k[0], k[1] + 1] for k in cells}
        x = base
        for _ in range(sweeps - 1):
            new = {}
            for h in range(h_n):
                plane = [x[t, h] for t in range(t_n)]
                lower, upper = from_lower(plane), from_upper(plane)
                for t in range(t_n):
                    k = (t, h)
                    local = (1.0 - relax_weight) * x[k] + base[k]
                    if h > 0:
                        local = local + height_lower[k] * x[t, h - 1]
                    if h < h_n - 1:
                        local = local + height_upper[k] * x[t, h + 1]
                    cast = (cast_lower[k] * pltpu.roll(x[k], 1, 0)
                            + cast_upper[k] * pltpu.roll(x[k], r - 1, 0))
                    new[k] = local + cast + (span_lower[k] * lower[t] + span_upper[k] * upper[t])
            x = new
        for t, h in cells:
            self.xa[t, h + 1, at, :] = x[t, h]

    def remainder(self, x, start, n, tiles, store, after=None):
        def body(h, k):
            centre, near = self.near(x, h, start, n, tiles)
            for t in range(tiles):
                store(t, h, near[t] - self.diag[t, h, pl.ds(start, n), :] * centre[t])
        self.loop(body, after)

    def keep_remainder(self, x, start, n):
        def store(t, h, value):
            self.rem[t, h, pl.ds(start, n), :] = value
        self.remainder(x, start, n, self.tiles, store)


def children(pieces):
    total = None
    for piece in pieces:
        total = piece if total is None else total + piece
    return total


def coarsen(fine, coarse, kind):
    half = fine.rows // 2
    key, lane = (lax.broadcasted_iota(jnp.int32, (LANES, LANES), d) for d in (0, 1))
    into = [as_matrix(lane == (key >> 1)), as_matrix(lane == 64 + (key >> 1))]
    ref, first = (fine.cb.at[0], PAD) if kind == 0 else (fine.rem, 0)
    scale = 0.125 * 0.25 if kind == 0 else 0.125
    for t in range(coarse.tiles):
        total = None
        for side in range(2):
            parts = [
                children(
                    ref[2 * t + side, plane, pl.ds(first + odd, half, stride=2), :]
                    for plane in (2 * h, 2 * h + 1) for odd in range(2)
                ) * scale
                for h in range(coarse.height)
            ]
            product = select_mm(jnp.concatenate(parts, axis=0), into[side])
            total = product if total is None else total + product
        coarse.cb[kind, t, :, PAD:PAD + half, :] = total.reshape(coarse.height, half, LANES)


def refine_add(coarse, x, fine, y, z, wide, start, n):
    half, first = n // 2, start // 2
    key, lane = (lax.broadcasted_iota(jnp.int32, (LANES, LANES), d) for d in (0, 1))
    out_of = [as_matrix(key == (lane >> 1)), as_matrix(key == 64 + (lane >> 1))]
    for t in range(coarse.tiles):
        stacked = x[t, 1:1 + coarse.height, PAD + first:PAD + first + half, :].reshape(coarse.height * half, LANES)
        for side in range(2):
            f = 2 * t + side
            product = select_mm(stacked, out_of[side]).reshape(coarse.height, half, LANES)
            for h in range(coarse.height):
                for odd in range(2):
                    wide[h, pl.ds(odd, half, stride=2), :] = product[h]
            for h in range(coarse.height):
                rows = wide[h, 0:n, :]
                for plane in (2 * h, 2 * h + 1):
                    at = pl.ds(PAD + start, n)
                    z[f, plane + 1, at, :] = y[f, plane + 1, at, :] + rows


def kernel(n_cast, n_span, levels, coeff_ref, source_ref, field_ref, residual_ref, *scratch):
    for i, level in enumerate(levels):
        level.bind(scratch[10 * i:10 * i + 10])
    l0, l1, l2, l3 = levels
    (edges, halos, half, small, packed, gathered, tall, wide0, wide2, load_sem,
     send_sem, recv_sem, send_c, recv_c, send_s, recv_s) = scratch[40:]
    c, s = lax.axis_index("cast"), lax.axis_index("span")
    height, rows, _ = coeff_ref.shape
    rows1, rows2 = rows // 2, rows // 4
    own = slice(PAD + rows, PAD + 2 * rows)
    load_coeff = pltpu.make_async_copy(coeff_ref, l0.cb.at[0, 0, :, own, :], load_sem.at[0])
    load_source = pltpu.make_async_copy(source_ref, l0.cb.at[1, 0, :, own, :], load_sem.at[1])
    load_coeff.start()
    load_source.start()

    def span_at(offset):
        return lax.rem(s + offset + n_span, n_span)

    def cast_at(offset):
        return lax.rem(c + offset + n_cast, n_cast)

    def blank(block):
        at = slice(PAD + block * rows, PAD + (block + 1) * rows)
        l0.cb[0, 0, :, at, :] = jnp.ones((height, rows, LANES), jnp.float32)
        l0.cb[1, 0, :, at, :] = jnp.zeros((height, rows, LANES), jnp.float32)
        within = slice(block * rows, (block + 1) * rows)
        for side in range(2):
            halos[0, side, :, within, :] = jnp.ones((2, rows, LANES), jnp.float32)
            halos[1, side, :, within, :] = jnp.zeros((2, rows, LANES), jnp.float32)

    @pl.when(c == 0)
    def _():
        blank(0)

    @pl.when(c == n_cast - 1)
    def _():
        blank(2)

    barrier = pltpu.get_barrier_semaphore()

    def greet(cast, span):
        pl.semaphore_signal(barrier, inc=1, device_id=(cast, span), device_id_type=MESH)

    for d in range(1, n_cast):
        greet(cast_at(d), s)
    for d in range(1, n_span):
        greet(c, span_at(d))

    @pl.when(c > 0)
    def _():
        greet(c - 1, span_at(1))
        greet(c - 1, span_at(-1))

    @pl.when(c < n_cast - 1)
    def _():
        greet(c + 1, span_at(1))
        greet(c + 1, span_at(-1))

    group = lane_iota(rows) >> 4

    def pack_edges(kind):
        for part in range(2):
            planes = [l0.cb[kind, 0, 8 * part + j, own, :] for j in range(8)]
            for side in range(2):
                merged = planes[0] if side == 0 else pltpu.roll(planes[0], 16, 1)
                for j in range(1, 8):
                    shift = (16 * j + 16 * side) % LANES
                    moved = pltpu.roll(planes[j], shift, 1) if shift else planes[j]
                    merged = jnp.where(group == j, moved, merged)
                edges[kind, side, part] = merged

    load_coeff.wait()
    pack_edges(0)
    load_source.wait()
    pack_edges(1)

    has_lower = lax.div(c + n_cast - 1, n_cast)
    has_upper = lax.div(2 * n_cast - 2 - c, n_cast)
    pl.semaphore_wait(barrier, n_cast + n_span - 2 + 2 * has_lower + 2 * has_upper)

    def block_copy(kind, dc):
        block = 1 - dc
        return pltpu.make_async_remote_copy(
            src_ref=l0.cb.at[kind, 0, :, pl.ds(PAD + rows, rows), :],
            dst_ref=l0.cb.at[kind, 0, :, pl.ds(PAD + block * rows, rows), :],
            send_sem=send_sem.at[kind, 6 + (dc + 1) // 2],
            recv_sem=recv_sem.at[kind, 6 + (dc + 1) // 2],
            device_id=(c + dc, s),
            device_id_type=MESH,
        )

    def edge_copy(kind, dc, side):
        return pltpu.make_async_remote_copy(
            src_ref=edges.at[kind, side],
            dst_ref=halos.at[kind, side, :, pl.ds((1 - dc) * rows, rows), :],
            send_sem=send_sem.at[kind, 3 * side + dc + 1],
            recv_sem=recv_sem.at[kind, 3 * side + dc + 1],
            device_id=(c + dc, span_at(2 * side - 1)),
            device_id_type=MESH,
        )

    def toward(kind, dc):
        return [block_copy(kind, dc), edge_copy(kind, dc, 0), edge_copy(kind, dc, 1)]

    def send_halo(kind):
        @pl.when(c < n_cast - 1)
        def _():
            for copy in toward(kind, 1):
                copy.start()

        @pl.when(c > 0)
        def _():
            for copy in toward(kind, -1):
                copy.start()

        edge_copy(kind, 0, 0).start()
        edge_copy(kind, 0, 1).start()

    first_half = lane_iota(3 * rows) < 64

    def take_halo(kind):
        edge_copy(kind, 0, 0).wait()
        edge_copy(kind, 0, 1).wait()

        @pl.when(c > 0)
        def _():
            for copy in toward(kind, 1):
                copy.wait_recv()
            for copy in toward(kind, -1):
                copy.wait_send()

        @pl.when(c < n_cast - 1)
        def _():
            for copy in toward(kind, -1):
                copy.wait_recv()
            for copy in toward(kind, 1):
                copy.wait_send()

        for part in range(2):
            above, beneath = halos[kind, 0, part], halos[kind, 1, part]
            for j in range(8):
                a = pltpu.roll(above, (LANES - 16 * j) % LANES, 1) if j else above
                b = pltpu.roll(beneath, 112 - 16 * j, 1) if j < 7 else beneath
                l0.cb[kind, 1, 8 * part + j, PAD:PAD + 3 * rows, :] = jnp.where(first_half, a, b)

    key, lane = (lax.broadcasted_iota(jnp.int32, (LANES, LANES), d) for d in (0, 1))
    narrow = as_matrix((lane == (key >> 1)) & (key < 64))
    quarter = lane_iota(rows2) >> 5

    def pack_own(kind, ref, first, scale):
        for h in range(l2.height):
            small[h] = children(
                ref[plane, pl.ds(first + odd, rows2, stride=2), :]
                for plane in (2 * h, 2 * h + 1) for odd in range(2)
            ) * scale
        product = select_mm(small[...].reshape(rows2 * l2.height, LANES), narrow)
        product = product.reshape(l2.height, rows2, LANES)
        merged = product[0]
        for h in range(1, l2.height):
            merged = merged + pltpu.roll(product[h], 32 * h, 1)
        packed[kind] = merged
        gathered[kind, s, c] = merged

    def along_cast(kind):
        return [pltpu.make_async_remote_copy(
            src_ref=packed.at[kind], dst_ref=gathered.at[kind, s, c],
            send_sem=send_c.at[kind, d - 1], recv_sem=recv_c.at[kind, d - 1],
            device_id=(cast_at(d), s), device_id_type=MESH) for d in range(1, n_cast)]

    def along_span(kind):
        return [pltpu.make_async_remote_copy(
            src_ref=gathered.at[kind, s], dst_ref=gathered.at[kind, s],
            send_sem=send_s.at[kind, d - 1], recv_sem=recv_s.at[kind, d - 1],
            device_id=(c, span_at(d)), device_id_type=MESH) for d in range(1, n_span)]

    def start(copies):
        for copy in copies:
            copy.start()

    def finished(copies):
        for copy in copies:
            copy.wait()

    def unpack(kind):
        for t in range(l2.tiles):
            for cc in range(n_cast):
                blocks = [gathered[kind, 4 * t + j, cc] for j in range(4)]
                for h in range(l2.height):
                    joined = None
                    for j in range(4):
                        shift = (32 * (j - h)) % LANES
                        moved = pltpu.roll(blocks[j], shift, 1) if shift else blocks[j]
                        joined = moved if joined is None else jnp.where(quarter == j, moved, joined)
                    at = PAD + rows2 * cc
                    l2.cb[kind, t, h, at:at + rows2, :] = joined

    send_halo(0)
    send_halo(1)
    stacked = jnp.concatenate([
        children(
            l0.cb[0, 0, plane, pl.ds(PAD + rows + odd, rows1, stride=2), :]
            for plane in (2 * h, 2 * h + 1) for odd in range(2)
        ) * (0.125 * 0.25)
        for h in range(l1.height)
    ], axis=0)
    half[...] = select_mm(stacked, as_matrix(lane == (key >> 1))).reshape(l1.height, rows1, LANES)
    pack_own(0, half, 0, 0.125 * 0.25)
    start(along_cast(0))
    for level in levels:
        level.clear_pads()
        level.clear_coeff_pads()
    tall[...] = jnp.zeros(tall.shape, jnp.float32)
    finished(along_cast(0))
    start(along_span(0))

    take_halo(0)
    l0.prepare(rows * c - rows, rows * n_cast)
    coarsen(l0, l1, 0)
    l1.prepare(rows1 * c - rows1, rows1 * n_cast)

    take_halo(1)
    l0.begin()
    l0.relax(l0.xa, l0.xb, 0, 3 * rows)
    l0.keep_remainder(l0.xb, 0, 3 * rows)
    coarsen(l0, l1, 1)
    l1.begin()
    l1.relax(l1.xa, l1.xb, 0, 3 * rows1)
    l1.keep_remainder(l1.xb, rows1, rows1)
    pack_own(1, l1.rem.at[0], rows1, 0.125)

    start(along_cast(1))
    finished(along_span(0))
    unpack(0)
    finished(along_cast(1))
    start(along_span(1))
    l2.prepare(0, l2.rows)
    coarsen(l2, l3, 0)
    l3.prepare(0, l3.rows)
    finished(along_span(1))
    unpack(1)

    l2.begin()
    l2.relax(l2.xa, l2.xb, 0, l2.rows)
    l2.keep_remainder(l2.xb, 0, l2.rows)
    coarsen(l2, l3, 1)
    l3.relax_held(COARSE)
    refine_add(l3, l3.xa, l2, l2.xb, l2.xa, wide2, 0, l2.rows)
    l2.relax(l2.xa, l2.xb, 0, l2.rows)
    l2.relax(l2.xb, l2.xa, 0, l2.rows)

    period = 64 * n_span
    place = jnp.where(lane < 96, lane, lane - LANES) + 64 * s
    place = jnp.where(place < 0, place + period, jnp.where(place >= period, place - period, place)) >> 1
    product = None
    for t in range(l2.tiles):
        stacked = l2.xa[t, 1:1 + l2.height, PAD:PAD + l2.rows, :].reshape(l2.height * l2.rows, LANES)
        term = select_mm(stacked, as_matrix(key + LANES * t == place))
        product = term if product is None else product + term
    product = product.reshape(l2.height, l2.rows, LANES)
    for h in range(l2.height):
        for odd in range(2):
            tall[h, pl.ds(PAD + odd, l2.rows, stride=2), :] = product[h]
    for h in range(l2.height):
        window = tall[h, pl.ds(pl.multiple_of(8 * c, 8), 3 * rows1), :]
        for plane in (2 * h, 2 * h + 1):
            l1.xa[0, plane + 1, PAD:PAD + 3 * rows1, :] = l1.xb[0, plane + 1, PAD:PAD + 3 * rows1, :] + window
    l1.relax(l1.xa, l1.xb, 0, 3 * rows1)
    l1.relax(l1.xb, l1.xa, 0, 3 * rows1)
    refine_add(l1, l1.xa, l0, l0.xb, l0.xa, wide0, rows - 8, rows + 16)
    l0.relax(l0.xa, l0.xb, rows - 8, rows + 16)
    l0.relax(l0.xb, l0.xa, rows - 8, rows + 16)

    save_field = pltpu.make_async_copy(
        l0.xa.at[0, pl.ds(1, height), pl.ds(PAD + rows, rows), :], field_ref, load_sem.at[0])
    save_field.start()

    def finish(t, h, value):
        residual_ref[h] = value

    l0.remainder(l0.xa, rows, rows, 1, finish)
    save_field.wait()


def solution(mesh):
    n_cast, n_span = mesh.shape["cast"], mesh.shape["span"]

    def shards(phase, viscosity_table, pressure_source):
        height, rows, width = phase.shape
        assert (height, rows, width) == (16, 16, LANES)
        levels = [
            Level(2, 16, 3 * rows, 4),
            Level(1, 8, 3 * rows // 2, 8),
            Level(n_span // 4, 4, 4 * n_cast, 4),
            Level(n_span // 8, 2, 2 * n_cast, 2),
        ]
        scratch = []
        for level in levels:
            scratch += level.scratch()
        dma = pltpu.SemaphoreType.DMA
        scratch += [
            pltpu.VMEM((2, 2, 2, rows, LANES), jnp.float32),
            pltpu.VMEM((2, 2, 2, 3 * rows, LANES), jnp.float32),
            pltpu.VMEM((8, 8, LANES), jnp.float32),
            pltpu.VMEM((4, 4, LANES), jnp.float32),
            pltpu.VMEM((2, 4, LANES), jnp.float32),
            pltpu.VMEM((2, n_span, n_cast, 4, LANES), jnp.float32),
            pltpu.VMEM((4, 8 * n_cast + 2 * PAD, LANES), jnp.float32),
            pltpu.VMEM((8, 3 * rows, LANES), jnp.float32),
            pltpu.VMEM((2, 4 * n_cast, LANES), jnp.float32),
            dma((2,)),
            dma((2, 8)), dma((2, 8)),
            dma((2, n_cast - 1)), dma((2, n_cast - 1)),
            dma((2, n_span - 1)), dma((2, n_span - 1)),
        ]
        kinds = lax.broadcasted_iota(jnp.int32, (3,) + phase.shape, 0)
        table = (1.0 / viscosity_table)[:, None, None, None]
        coeff = jnp.sum(jnp.where(kinds == phase[None], table, 0.0), axis=0)
        block = jax.ShapeDtypeStruct(phase.shape, jnp.float32)
        anywhere = pl.BlockSpec(memory_space=pl.ANY)
        vmem = pl.BlockSpec(memory_space=pltpu.VMEM)
        return pl.pallas_call(
            functools.partial(kernel, n_cast, n_span, levels),
            out_shape=(block, block),
            in_specs=[anywhere, anywhere],
            out_specs=(vmem, vmem),
            scratch_shapes=scratch,
            compiler_params=pltpu.CompilerParams(
                collective_id=0, has_side_effects=True, vmem_limit_bytes=40 * 2**20
            ),
        )(coeff, pressure_source)

    placed = P(None, "cast", "span")
    return jax.shard_map(
        shards, mesh=mesh, in_specs=(placed, P(), placed), out_specs=(placed, placed), check_vma=False
    )
```
